256 devices in a mesh: dp: 64 (over z, y, core), group: 4 (over x).
Axes of the slice: x: 4, y: 4, z: 8, core: 2. Of those that a mesh axis runs over, the one named last changes fastest.
Arguments:
- acts: bfloat16 [32768, 2048], P('dp'), may hold values from -6 to 6
- grad_out: bfloat16 [32768, 8192], P('dp', 'group'), may hold values from -700 to 700
- projector: bfloat16 [2048, 256], P('dp'), may hold values from -0.125 to 0.125
- moment_one: float32 [256, 8192], P(None, 'group'), may hold values from -6 to 6
- moment_two: float32 [256, 8192], P(None, 'group'), may hold values from 0.25 to 4
Outputs:
- update: float32 [2048, 8192], P('dp', 'group')
- moment_one_new: float32 [256, 8192], P(None, 'group')
- moment_two_new: float32 [256, 8192], P(None, 'group')
The draws below stay inside these ranges and needn't reach their ends.
All inputs are finite; a program needn't handle non-finite values.
Results may differ from the reference program's by a relative error of at most 0.00035.
Values may be sent and summed in bfloat16 or wider, within the bound.
A program may use at most 128 MiB of HBM per device.

```python
import math
import jax
import jax.numpy as jnp
from jax import lax

D = 2048
FF = 8192
RANK = 256
TOKENS = 32768


def draw_grad_out(key, part):
    key = jax.random.fold_in(key, 7)
    key_base, key_cols, key_rows = jax.random.split(key, 3)
    position = jnp.arange(FF, dtype=jnp.float32) / FF
    base = jnp.clip(jax.random.normal(key_base, (TOKENS, FF), jnp.float32), -5.0, 5.0)
    ramp = 3.0 ** (0.75 * position)
    col_scale = jnp.exp(jax.random.uniform(key_cols, (1, FF), jnp.float32) * jnp.log(10.0))
    row_scale = jnp.exp(jax.random.uniform(key_rows, (TOKENS, 1), jnp.float32) * jnp.log(4.0))
    return (base * ramp[None, :] * col_scale * row_scale).astype(jnp.bfloat16)


def block_scale(key, extent, cuts, smallest, high):
    level = 1.0
    for dim, shards_of in cuts:
        heights = jax.random.uniform(jax.random.fold_in(jax.random.fold_in(key, 6), dim), (shards_of,), jnp.float32, smallest / len(cuts), high / len(cuts))
        level = level * jnp.repeat(jnp.exp(heights), extent[dim] // shards_of).reshape((-1,) + (1,) * (len(extent) - 1 - dim))
    return level


def bell_draw(stream_key, extent, deviation, most, cuts=(), kind=jnp.bfloat16):
    values = jax.random.normal(stream_key, extent, jnp.float32) * deviation
    if len(cuts) > 0:
        values = block_scale(stream_key, extent, cuts, -0.22, 0.18) * values
    return jnp.clip(values, min=-most, max=most).astype(kind)


def setup_inputs(seed: int = 0) -> dict:
    splits = jax.random.split(jax.random.key(seed), 6)
    return {
        "acts": bell_draw(splits[0], (TOKENS, D), 1.0, 6.0, ((0, 64),)),
        "grad_out": draw_grad_out(jax.random.fold_in(splits[5], 71), 0),
        "projector": bell_draw(splits[2], (D, RANK), D ** -0.5, 0.125, ((0, 64),)),
        "moment_one": bell_draw(splits[3], (RANK, FF), 1.0, 6.0, ((1, 4),), jnp.float32),
        "moment_two": jnp.clip(jnp.exp(math.log(4.0) - 2.7725887 * jax.random.uniform(splits[4], (RANK, FF), jnp.float32) ** block_scale(splits[4], (RANK, FF), ((1, 4),), -0.2, 0.2)), 0.25, 4.0),
    }


beta_one = 0.9
beta_two = 0.95
bias_one = 1.0 - 0.9 ** 10
bias_two = 1.0 - 0.95 ** 10
galore_scale = 0.25

def reference(acts, grad_out, projector, moment_one, moment_two):
    block = math.gcd(TOKENS, 4096)
    count = TOKENS // block
    act_blocks = acts.reshape(count, block, D)
    grad_blocks = grad_out.reshape(count, block, FF)
    projector_wide = projector.astype(jnp.float32)

    def accumulate(total, pair):
        act_block, grad_block = pair
        along = jnp.dot(act_block.astype(jnp.float32), projector_wide, precision=lax.Precision.HIGHEST)
        total = total + jnp.dot(along.T, grad_block.astype(jnp.float32), precision=lax.Precision.HIGHEST)
        return (total, None)
    proj, _ = lax.scan(accumulate, jnp.zeros((RANK, FF), jnp.float32), (act_blocks, grad_blocks))
    energy = jnp.sum(proj * proj)
    clip = jnp.minimum(1.0, 1.0 / jnp.sqrt(energy / (RANK * FF) + 1e-06))
    clipped = clip * proj
    first = beta_one * moment_one + (1.0 - beta_one) * clipped
    second = beta_two * moment_two + (1.0 - beta_two) * clipped * clipped
    direction = first / bias_one / (jnp.sqrt(second / bias_two) + 1e-08)
    update = galore_scale * jnp.dot(projector_wide, direction, precision=lax.Precision.HIGHEST)
    return (update, first, second)
```

```python
import functools
import math

import jax
import jax.numpy as jnp
from jax import lax
from jax.experimental import pallas as pl
from jax.experimental.pallas import tpu as pltpu
from jax.sharding import PartitionSpec as P

beta_one = 0.9
beta_two = 0.95
bias_one = 1.0 - 0.9**10
bias_two = 1.0 - 0.95**10
galore_scale = 0.25

MESH = pl.DeviceIdType.MESH
NZ, NY, NX = 8, 4, 4
SPAN = 250.0
HALF = 125.0
LN2 = math.log(2.0)
NEAR = (0, 1, 7, 2, 6, 3, 5, 4)
FAR = (4, 3, 5, 2, 6, 1, 7, 0)
f32 = jnp.float32
bf16 = jnp.bfloat16


def tiles_of(block):
    return [block[16 * r : 16 * r + 16, 128 * l : 128 * l + 128] for r in range(2) for l in range(2)]


def encode(tiles, packet):
    top = functools.reduce(jnp.maximum, [jnp.abs(t) for t in tiles])
    top = jnp.max(top, axis=0, keepdims=True)
    scale = (jnp.maximum(top, 1e-30) * 1.01).astype(bf16)
    packet[4] = jnp.broadcast_to(scale, (16, 128))
    rate = SPAN / scale.astype(f32)
    for i, t in enumerate(tiles):
        size = jnp.exp2(jnp.abs(t) * rate - HALF)
        packet[i] = jnp.where(t < 0, -size, size).astype(bf16)


def decode(packet):
    rate = packet[4].astype(f32) * (1.0 / (SPAN * LN2))
    out = []
    for i in range(4):
        code = packet[i].astype(f32)
        size = (jnp.log(jnp.abs(code)) + HALF * LN2) * rate
        out.append(jnp.where(code < 0, -size, size))
    return out


def reduce_kernel(
    acts, grad, p_ref, proj_out, energy_out,
    a_all, g_all, p_all, along, lhs, part, y_send, y_recv, z_send, z_recv, gathered, energies,
    load_sem, pair_send, pair_recv, pz_send, pz_recv, py_send, py_recv,
    ry_send, ry_recv, rz_send, rz_recv, az_send, az_recv, ay_send, ay_recv, ac_send, ac_recv, e_send, e_recv,
):
    dp = lax.axis_index("dp")
    x = lax.axis_index("group")
    c = lax.rem(dp, 2)
    y = lax.rem(lax.div(dp, 2), NY)
    z = lax.div(dp, 2 * NY)

    def at(zz, yy, cc, xx):
        return ((zz * NY + yy) * 2 + cc, xx)

    def zoff(d):
        return lax.rem(z + d, NZ)

    def yoff(d):
        return lax.rem(y + d, NY)

    def remote(src, dst, send, recv, device):
        return pltpu.make_async_remote_copy(
            src_ref=src, dst_ref=dst, send_sem=send, recv_sem=recv, device_id=device, device_id_type=MESH
        )

    me = at(z, y, c, x)
    sibling = at(z, y, 1 - c, x)
    loads = [
        pltpu.make_async_copy(acts, a_all.at[pl.ds(0, 512)], load_sem.at[0]),
        pltpu.make_async_copy(grad, g_all.at[pl.ds(0, 512)], load_sem.at[1]),
    ]
    for copy in loads:
        copy.start()

    barrier = pltpu.get_barrier_semaphore()
    peers = [at(zoff(d), y, cc, x) for d in range(1, NZ) for cc in range(2)]
    peers += [at(z, yoff(d), c, x) for d in range(1, NY)] + [sibling]
    peers += [at(z, y, c, lax.rem(x + d, NX)) for d in range(1, NX)]
    for peer in peers:
        pl.semaphore_signal(barrier, inc=1, device_id=peer, device_id_type=MESH)
    pl.semaphore_wait(barrier, len(peers))

    mine = pl.ds(pl.multiple_of((z * NY + y) * 64 + c * 32, 32), 32)
    for d in NEAR[::-1]:
        for cc in range(2):
            src = p_ref.at[:, pl.ds(cc * 128, 128)]
            if d:
                remote(src, p_all.at[mine], pz_send, pz_recv.at[d], at(zoff(d), y, cc, x)).start()
    for cc in range(2):

        @pl.when(c != cc)
        def _():
            remote(p_ref.at[:, pl.ds(cc * 128, 128)], p_all.at[mine], pz_send, pz_recv.at[0], sibling).start()

        @pl.when(c == cc)
        def _():
            p_all[mine, :] = p_ref[:, cc * 128 : cc * 128 + 128]

    pair = [
        remote(acts, a_all.at[pl.ds(512, 512)], pair_send.at[0], pair_recv.at[0], sibling),
        remote(grad, g_all.at[pl.ds(512, 512)], pair_send.at[1], pair_recv.at[1], sibling),
    ]
    for copy in pair:
        copy.start()

    def p_rows(zz, yy, n=64):
        return pl.ds(pl.multiple_of((zz * NY + yy) * 64, 64), n)

    def p_forward(d):
        zz = zoff(NZ - d)
        if d:
            remote(p_all.at[p_rows(zz, y)], p_all.at[p_rows(zz, y)], pz_send, pz_recv.at[d], me).wait_recv()
        else:
            remote(p_all.at[pl.ds(0, 32)], p_all.at[pl.ds(0, 32)], pz_send, pz_recv.at[0], me).wait_recv()
        for dy in range(1, NY):
            remote(
                p_all.at[p_rows(zz, y)], p_all.at[p_rows(zz, y)], py_send, py_recv.at[d], at(z, yoff(dy), c, x)
            ).start()

    def p_use(d, first):
        zz = zoff(NZ - d)
        three = p_all.at[pl.ds(0, 192)]
        remote(three, three, py_send, py_recv.at[d], me).wait_recv()
        if first:
            loads[0].wait()
            pair[0].wait_recv()
        cols = pl.ds(pl.multiple_of(zz * 256, 256), 256)
        term = jnp.dot(a_all[:, cols], p_all[p_rows(zz, 0, 256), :], preferred_element_type=f32)
        if first:
            along[...] = term
        else:
            along[...] += term

    lag = 3
    for k in range(NZ + lag):
        if k < NZ:
            p_forward(NEAR[k])
        if k >= lag:
            p_use(NEAR[k - lag], k == lag)

    turned = along[...].T
    high = turned.astype(bf16)
    lhs[pl.ds(0, 128), :] = high
    lhs[pl.ds(128, 128), :] = (turned - high.astype(f32)).astype(bf16)
    loads[1].wait()
    pair[1].wait_recv()

    for k, d in enumerate(FAR):
        cols = pl.ds(pl.multiple_of(zoff(d) * 256, 256), 256)
        both = jnp.dot(lhs[...], g_all[:, cols], preferred_element_type=f32)
        part[k] = both[:128] + both[128:]
        for dy in range(1, NY):
            yy = yoff(dy)
            encode(tiles_of(part[k, pl.ds(pl.multiple_of(yy * 32, 32), 32), :]), y_send.at[k, dy - 1])
            remote(y_send.at[k, dy - 1], y_recv.at[k, dy - 1], ry_send, ry_recv.at[k], at(z, yy, c, x)).start()

    all_p = p_all.at[pl.ds(0, 480)]
    remote(all_p, all_p, pz_send, pz_recv.at[0], me).wait_send()
    all_p = p_all.at[pl.ds(0, 1536)]
    remote(all_p, all_p, py_send, py_recv.at[0], me).wait_send()
    for copy in pair:
        copy.wait_send()

    own = pl.ds(pl.multiple_of(y * 32, 32), 32)
    total = None
    for k, d in enumerate(FAR):
        remote(y_recv.at[k], y_recv.at[k], ry_send, ry_recv.at[k], me).wait_recv()
        tiles = tiles_of(part[k, own, :])
        for i in range(NY - 1):
            tiles = [a + b for a, b in zip(tiles, decode(y_recv.at[k, i]))]
        if d:
            encode(tiles, z_send.at[d - 1])
            remote(z_send.at[d - 1], z_recv.at[d - 1], rz_send, rz_recv.at[d], at(zoff(d), y, c, x)).start()
        else:
            total = tiles
    for d in NEAR[1:]:
        remote(z_recv.at[d - 1], z_recv.at[d - 1], rz_send, rz_recv.at[d], me).wait_recv()
        total = [a + b for a, b in zip(total, decode(z_recv.at[d - 1]))]

    encode(total, gathered.at[c, z, y])
    for d in NEAR[:0:-1]:
        remote(
            gathered.at[c, z, y], gathered.at[c, z, y], az_send, az_recv.at[d], at(zoff(d), y, c, x)
        ).start()

    def out_forward(d):
        zz = zoff(NZ - d)
        block = gathered.at[c, zz, y]
        if d:
            remote(block, block, az_send, az_recv.at[d], me).wait_recv()
        for dy in range(1, NY):
            remote(block, block, ay_send, ay_recv.at[d], at(z, yoff(dy), c, x)).start()

    def out_share(d):
        zz = zoff(NZ - d)
        three = gathered.at[c, zz, pl.ds(0, 3)]
        remote(three, three, ay_send, ay_recv.at[d], me).wait_recv()
        remote(gathered.at[c, zz], gathered.at[c, zz], ac_send, ac_recv.at[d], sibling).start()

    for k in range(NZ + lag):
        if k < NZ:
            out_forward(NEAR[k])
        if k >= lag:
            out_share(NEAR[k - lag])

    energies[0] = jnp.zeros((8, 128), f32)

    def unpack(cc, zz):
        energy = energies[0]
        for yy in range(NY):
            tiles = decode(gathered.at[cc, zz, yy])
            for i, t in enumerate(tiles):
                rows = pl.ds(pl.multiple_of(cc * 128 + yy * 32 + (i // 2) * 16, 16), 16)
                cols = pl.ds(pl.multiple_of(zz * 256 + (i % 2) * 128, 128), 128)
                proj_out[rows, cols] = t
                square = t * t
                energy = energy + square[:8] + square[8:]
        energies[0] = energy

    def unpack_own(zz, carry):
        unpack(c, zz)
        return carry

    lax.fori_loop(0, NZ, unpack_own, 0)
    for d in NEAR:
        zz = zoff(NZ - d)
        theirs = gathered.at[1 - c, zz]
        remote(theirs, theirs, ac_send, ac_recv.at[d], me).wait_recv()
        unpack(1 - c, zz)

    for d in range(1, NX):
        remote(
            energies.at[0], energies.at[d], e_send.at[d], e_recv.at[d], at(z, y, c, lax.rem(x + d, NX))
        ).start()
    all_y = y_send
    remote(all_y, all_y, ry_send, ry_recv.at[0], me).wait_send()
    remote(z_send, z_send, rz_send, rz_recv.at[1], me).wait_send()
    seven = z_send
    remote(seven, seven, az_send, az_recv.at[1], me).wait_send()
    many = gathered.at[0, pl.ds(0, 6)]
    remote(many, many, ay_send, ay_recv.at[0], me).wait_send()
    many = gathered.at[0]
    remote(many, many, ac_send, ac_recv.at[0], me).wait_send()
    energy = energies[0]
    for d in range(1, NX):
        remote(energies.at[0], energies.at[d], e_send.at[d], e_recv.at[d], me).wait()
        energy = energy + energies[d]
    energy_out[...] = energy


def reduced(acts, grad_out, projector):
    sem = pltpu.SemaphoreType.DMA
    any_space = pl.BlockSpec(memory_space=pl.ANY)
    vmem = pl.BlockSpec(memory_space=pltpu.VMEM)
    return pl.pallas_call(
        reduce_kernel,
        name="projected_gradient",
        out_shape=(jax.ShapeDtypeStruct((256, 2048), f32), jax.ShapeDtypeStruct((8, 128), f32)),
        in_specs=[any_space, any_space, vmem],
        out_specs=(vmem, vmem),
        scratch_shapes=[
            pltpu.VMEM((1024, 2048), bf16),
            pltpu.VMEM((1024, 2048), bf16),
            pltpu.VMEM((2048, 128), bf16),
            pltpu.VMEM((1024, 128), f32),
            pltpu.VMEM((256, 1024), bf16),
            pltpu.VMEM((NZ, 128, 256), f32),
            pltpu.VMEM((NZ, NY - 1, 5, 16, 128), bf16),
            pltpu.VMEM((NZ, NY - 1, 5, 16, 128), bf16),
            pltpu.VMEM((NZ - 1, 5, 16, 128), bf16),
            pltpu.VMEM((NZ - 1, 5, 16, 128), bf16),
            pltpu.VMEM((2, NZ, NY, 5, 16, 128), bf16),
            pltpu.VMEM((NX, 8, 128), f32),
            sem((2,)), sem((2,)), sem((2,)),
            sem, sem((NZ,)), sem, sem((NZ,)),
            sem, sem((NZ,)), sem, sem((NZ,)),
            sem, sem((NZ,)), sem, sem((NZ,)), sem, sem((NZ,)),
            sem((NX,)), sem((NX,)),
        ],
        compiler_params=pltpu.CompilerParams(
            collective_id=0, has_side_effects=True, vmem_limit_bytes=32 * 1024 * 1024
        ),
        cost_estimate=pl.CostEstimate(flops=1 << 31, bytes_accessed=6 << 20, transcendentals=1 << 20),
    )(acts, grad_out, projector)


def update_kernel(entries, proj, energy, projector, first_old, second_old, update, first_new, second_new):
    mean = jnp.sum(energy[...]) / entries
    clip = jnp.minimum(1.0, 1.0 / jnp.sqrt(jnp.full((1, 128), mean + 1e-06, f32)))
    clip = jnp.concatenate([clip, clip], axis=1)
    clipped = clip * proj[...]
    first = beta_one * first_old[...] + (1.0 - beta_one) * clipped
    second = beta_two * second_old[...] + (1.0 - beta_two) * clipped * clipped
    first_new[...] = first
    second_new[...] = second
    direction = first * (1.0 / bias_one) / (jnp.sqrt(second * (1.0 / bias_two)) + 1e-08)
    high = direction.astype(bf16)
    low = (direction - high.astype(f32)).astype(bf16)
    rows = projector[...]
    moved = jnp.dot(rows, high, preferred_element_type=f32) + jnp.dot(rows, low, preferred_element_type=f32)
    update[...] = galore_scale * moved


def updated(proj, energy, projector, moment_one, moment_two, entries):
    wide = pl.BlockSpec((256, 256), lambda i: (0, i))
    return pl.pallas_call(
        functools.partial(update_kernel, entries),
        name="adam_update",
        grid=(8,),
        out_shape=(
            jax.ShapeDtypeStruct((32, 2048), f32),
            jax.ShapeDtypeStruct((256, 2048), f32),
            jax.ShapeDtypeStruct((256, 2048), f32),
        ),
        in_specs=[
            wide,
            pl.BlockSpec((8, 128), lambda i: (0, 0)),
            pl.BlockSpec((32, 256), lambda i: (0, 0)),
            wide,
            wide,
        ],
        out_specs=(pl.BlockSpec((32, 256), lambda i: (0, i)), wide, wide),
        cost_estimate=pl.CostEstimate(flops=1 << 26, bytes_accessed=10 << 20, transcendentals=1 << 20),
    )(proj, energy, projector, moment_one, moment_two)


def on_device(acts, grad_out, projector, moment_one, moment_two):
    entries = float(projector.shape[1] * grad_out.shape[1] * NX)
    proj, energy = reduced(acts, grad_out, projector)
    return updated(proj, energy, projector, moment_one, moment_two, entries)


def solution(mesh):
    placed = (P("dp", None), P("dp", "group"), P("dp", None), P(None, "group"), P(None, "group"))
    return jax.shard_map(
        on_device,
        mesh=mesh,
        in_specs=placed,
        out_specs=(P("dp", "group"), P(None, "group"), P(None, "group")),
        check_vma=False,
    )
```

```python
import functools
import math

import jax
import jax.numpy as jnp
from jax import lax
from jax.experimental import pallas as pl
from jax.experimental.pallas import tpu as pltpu
from jax.sharding import PartitionSpec as P

beta_one = 0.9
beta_two = 0.95
bias_one = 1.0 - 0.9**10
bias_two = 1.0 - 0.95**10
galore_scale = 0.25

MESH = pl.DeviceIdType.MESH
NZ, NY, NX = 8, 4, 4
SPAN = 250.0
HALF = 125.0
LN2 = math.log(2.0)
NEAR = (0, 1, 7, 2, 6, 3, 5, 4)
FAR = (4, 3, 5, 2, 6, 1, 7, 0)
f32 = jnp.float32
bf16 = jnp.bfloat16


def tiles_of(block):
    return [block[16 * r : 16 * r + 16, 128 * l : 128 * l + 128] for r in range(2) for l in range(2)]


def scale_of(tiles):
    top = functools.reduce(jnp.maximum, [jnp.abs(t) for t in tiles])
    top = jnp.max(top, axis=0, keepdims=True)
    return (jnp.maximum(top, 1e-30) * 1.01).astype(bf16).astype(f32)


def encode(tiles, scale):
    rate = SPAN / scale
    out = []
    for t in tiles:
        size = jnp.exp2(jnp.abs(t) * rate - HALF)
        out.append(jnp.where(t < 0, -size, size).astype(bf16))
    return out


def decode(codes, scale):
    rate = scale * (1.0 / (SPAN * LN2))
    out = []
    for code in codes:
        code = code.astype(f32)
        size = (jnp.log(jnp.abs(code)) + HALF * LN2) * rate
        out.append(jnp.where(code < 0, -size, size))
    return out


def reduce_kernel(
    entries, acts, grad, p_hbm, proj_out, clip_out,
    p_ref, a_all, g_all, p_all, along, lhs, part, y_send, y_recv, z_send, z_recv, gathered, sums,
    load_sem, pair_send, pair_recv, pz_send, pz_recv, py_send, py_recv,
    ry_send, ry_recv, rz_send, rz_recv, az_send, az_recv, ay_send, ay_recv, ac_send, ac_recv,
    ex_send, ex_recv, ey_send, ey_recv,
):
    dp = lax.axis_index("dp")
    x = lax.axis_index("group")
    c = lax.rem(dp, 2)
    y = lax.rem(lax.div(dp, 2), NY)
    z = lax.div(dp, 2 * NY)

    def at(zz, yy, cc, xx):
        return ((zz * NY + yy) * 2 + cc, xx)

    def zoff(d):
        return lax.rem(z + d, NZ)

    def yoff(d):
        return lax.rem(y + d, NY)

    def xoff(d):
        return lax.rem(x + d, NX)

    def remote(src, dst, send, recv, device):
        return pltpu.make_async_remote_copy(
            src_ref=src, dst_ref=dst, send_sem=send, recv_sem=recv, device_id=device, device_id_type=MESH
        )

    me = at(z, y, c, x)
    sibling = at(z, y, 1 - c, x)

    def arrived(ref, recv):
        remote(ref, ref, pz_send, recv, me).wait_recv()

    def sent(ref, send):
        remote(ref, ref, send, pz_recv.at[0], me).wait_send()

    loads = [
        pltpu.make_async_copy(p_hbm, p_ref, load_sem.at[2]),
        pltpu.make_async_copy(acts, a_all.at[pl.ds(0, 512)], load_sem.at[0]),
        pltpu.make_async_copy(grad, g_all.at[pl.ds(0, 512)], load_sem.at[1]),
    ]
    for copy in loads:
        copy.start()

    barrier = pltpu.get_barrier_semaphore()
    peers = [at(zoff(d), y, cc, x) for d in NEAR[:0:-1] for cc in range(2)]
    peers += [at(z, yoff(d), cc, x) for d in range(1, NY) for cc in range(2)] + [sibling]
    peers += [at(z, y, c, xoff(d)) for d in range(1, NX)]
    for peer in peers:
        pl.semaphore_signal(barrier, inc=1, device_id=peer, device_id_type=MESH)
    loads[0].wait()
    pl.semaphore_wait(barrier, len(peers))

    mine = pl.ds(pl.multiple_of((z * NY + y) * 64 + c * 32, 32), 32)
    for cc in range(2):

        @pl.when(c != cc)
        def _():
            remote(p_ref.at[:, pl.ds(cc * 128, 128)], p_all.at[mine], pz_send, pz_recv.at[0], sibling).start()

        @pl.when(c == cc)
        def _():
            p_all[mine, :] = p_ref[:, cc * 128 : cc * 128 + 128]

    for d in NEAR[:0:-1]:
        for cc in range(2):
            src = p_ref.at[:, pl.ds(cc * 128, 128)]
            remote(src, p_all.at[mine], pz_send, pz_recv.at[d], at(zoff(d), y, cc, x)).start()

    pair = [
        remote(acts, a_all.at[pl.ds(512, 512)], pair_send.at[0], pair_recv.at[0], sibling),
        remote(grad, g_all.at[pl.ds(512, 512)], pair_send.at[1], pair_recv.at[1], sibling),
    ]
    for copy in pair:
        copy.start()

    def p_rows(zz, yy, n=64):
        return pl.ds(pl.multiple_of((zz * NY + yy) * 64, 64), n)

    def p_forward(d):
        chunk = p_all.at[p_rows(zoff(NZ - d), y)]
        arrived(chunk if d else p_all.at[pl.ds(0, 32)], pz_recv.at[d])
        for dy in (2, 1, 3):
            remote(chunk, chunk, py_send, py_recv.at[d], at(z, yoff(dy), c, x)).start()

    def p_use(d, first):
        zz = zoff(NZ - d)
        arrived(p_all.at[pl.ds(0, 192)], py_recv.at[d])
        if first:
            loads[1].wait()
            pair[0].wait_recv()
        cols = pl.ds(pl.multiple_of(zz * 256, 256), 256)
        term = jnp.dot(a_all[:, cols], p_all[p_rows(zz, 0, 256), :], preferred_element_type=f32)
        if first:
            along[...] = term
        else:
            along[...] += term

    lag = 4
    for k in range(NZ + lag):
        if k < NZ:
            p_forward(NEAR[k])
        if k >= lag:
            p_use(NEAR[k - lag], k == lag)

    turned = along[...].T
    high = turned.astype(bf16)
    lhs[pl.ds(0, 128), :] = high
    lhs[pl.ds(128, 128), :] = (turned - high.astype(f32)).astype(bf16)
    loads[2].wait()
    pair[1].wait_recv()

    row = lax.broadcasted_iota(jnp.int32, (16, 128), 0)
    for k, d in enumerate(FAR):
        cols = pl.ds(pl.multiple_of(zoff(d) * 256, 256), 256)
        both = jnp.dot(lhs[...], g_all[:, cols], preferred_element_type=f32)
        part[k] = both[:128] + both[128:]
        if k % 2 == 0:
            continue
        for dy in (2, 1, 3):
            yy = yoff(dy)
            message = y_send.at[k // 2, dy - 1]
            scales = []
            for j in range(2):
                tiles = tiles_of(part[k - 1 + j, pl.ds(pl.multiple_of(yy * 32, 32), 32), :])
                scales.append(scale_of(tiles))
                for i, code in enumerate(encode(tiles, scales[j])):
                    message[4 * j + i] = code
            message[8] = jnp.where(row < 8, scales[0], scales[1]).astype(bf16)
            remote(
                message, y_recv.at[k // 2, dy - 1], ry_send, ry_recv.at[k // 2], at(z, yy, c, x)
            ).start()

    sent(p_all.at[pl.ds(0, 480)], pz_send)
    sent(p_all.at[pl.ds(0, 1536)], py_send)
    for copy in pair:
        copy.wait_send()

    own = pl.ds(pl.multiple_of(y * 32, 32), 32)
    for k, d in enumerate(FAR):
        if k % 2 == 0:
            arrived(y_recv.at[k // 2], ry_recv.at[k // 2])
        total = tiles_of(part[k, own, :])
        for i in range(NY - 1):
            message = y_recv.at[k // 2, i]
            scale = message[8][8 * (k % 2) : 8 * (k % 2) + 1].astype(f32)
            codes = [message[4 * (k % 2) + j] for j in range(4)]
            total = [a + b for a, b in zip(total, decode(codes, scale))]
        if d:
            packet = z_send.at[d - 1]
            scale = scale_of(total)
            for i, code in enumerate(encode(total, scale)):
                packet[i] = code
            packet[4] = jnp.broadcast_to(scale, (16, 128)).astype(bf16)
            remote(packet, z_recv.at[d - 1], rz_send, rz_recv.at[d], at(zoff(d), y, c, x)).start()
    sent(y_send, ry_send)
    for d in NEAR[1:]:
        packet = z_recv.at[d - 1]
        arrived(packet, rz_recv.at[d])
        codes = [packet[j] for j in range(4)]
        total = [a + b for a, b in zip(total, decode(codes, packet[4][:1].astype(f32)))]

    packet = gathered.at[c, z, y]
    scale = scale_of(total)
    energy = jnp.sum(functools.reduce(jnp.add, [t * t for t in total]), axis=0, keepdims=True)
    e_high = energy.astype(bf16).astype(f32)
    e_mid = (energy - e_high).astype(bf16).astype(f32)
    e_low = energy - e_high - e_mid
    for i, code in enumerate(encode(total, scale)):
        packet[i] = code
    last = jnp.where(row < 8, scale, 0.0)
    for i, part_of in enumerate((e_high, e_mid, e_low)):
        last = jnp.where(row == 8 + i, part_of, last)
    packet[4] = last.astype(bf16)
    for d in NEAR[:0:-1]:
        remote(packet, packet, az_send, az_recv.at[d], at(zoff(d), y, c, x)).start()

    def out_forward(d):
        block = gathered.at[c, zoff(NZ - d), y]
        if d:
            arrived(block, az_recv.at[d])
        for dy in (2, 1, 3):
            remote(block, block, ay_send, ay_recv.at[d], at(z, yoff(dy), c, x)).start()

    def out_share(d):
        zz = zoff(NZ - d)
        arrived(gathered.at[c, zz, pl.ds(0, 3)], ay_recv.at[d])
        remote(gathered.at[c, zz], gathered.at[c, zz], ac_send, ac_recv.at[d], sibling).start()

    for k in range(NZ):
        out_forward(NEAR[k])
    sent(z_send, rz_send)

    tile = functools.reduce(jnp.add, [gathered[c, zz, y, 4].astype(f32) for zz in range(NZ)])
    sums[0] = jnp.where(lax.broadcasted_iota(jnp.int32, (8, 128), 0) < 3, tile[8:], 0.0)
    for d in (2, 1, 3):
        remote(sums.at[0], sums.at[d], ex_send, ex_recv, at(z, y, c, xoff(d))).start()
    for k in range(NZ // 2):
        out_share(NEAR[k])
    arrived(sums.at[pl.ds(0, 3)], ex_recv)
    sums[4] = sums[0] + sums[1] + sums[2] + sums[3]
    slot = 5
    for dy in (2, 1, 3, 0):
        for dc in (1, 0):
            if dy or dc:
                cc = lax.rem(c + dc, 2)
                remote(sums.at[4], sums.at[slot], ey_send, ey_recv, at(z, yoff(dy), cc, x)).start()
                slot += 1
    for k in range(NZ // 2, NZ):
        out_share(NEAR[k])

    def unpack(cc, zz):
        for yy in range(NY):
            source = gathered.at[cc, zz, yy]
            codes = [source[j] for j in range(4)]
            for i, t in enumerate(decode(codes, source[4][:1].astype(f32))):
                rows = pl.ds(pl.multiple_of(cc * 128 + yy * 32 + (i // 2) * 16, 16), 16)
                cols = pl.ds(pl.multiple_of(zz * 256 + (i % 2) * 128, 128), 128)
                proj_out[rows, cols] = t

    def unpack_own(zz, carry):
        unpack(c, zz)
        return carry

    lax.fori_loop(0, NZ, unpack_own, 0)
    arrived(sums.at[pl.ds(0, 7)], ey_recv)
    energy = functools.reduce(jnp.add, [sums[i] for i in range(4, 12)])
    mean = jnp.full((8, 128), jnp.sum(energy) / entries + 1e-06, f32)
    clip_out[...] = jnp.minimum(1.0, 1.0 / jnp.sqrt(mean))
    for d in NEAR:
        zz = zoff(NZ - d)
        arrived(gathered.at[1 - c, zz], ac_recv.at[d])
        unpack(1 - c, zz)

    sent(z_send, az_send)
    sent(gathered.at[0, pl.ds(0, 6)], ay_send)
    sent(gathered.at[0], ac_send)
    sent(sums.at[pl.ds(0, 3)], ex_send)
    sent(sums.at[pl.ds(0, 7)], ey_send)


def reduced(acts, grad_out, projector, entries):
    sem = pltpu.SemaphoreType.DMA
    hbm = pl.BlockSpec(memory_space=pltpu.HBM)
    vmem = pl.BlockSpec(memory_space=pltpu.VMEM)
    return pl.pallas_call(
        functools.partial(reduce_kernel, entries),
        name="projected_gradient",
        out_shape=(jax.ShapeDtypeStruct((256, 2048), f32), jax.ShapeDtypeStruct((8, 128), f32)),
        in_specs=[hbm, hbm, hbm],
        out_specs=(vmem, vmem),
        scratch_shapes=[
            pltpu.VMEM((32, 256), bf16),
            pltpu.VMEM((1024, 2048), bf16),
            pltpu.VMEM((1024, 2048), bf16),
            pltpu.VMEM((2048, 128), bf16),
            pltpu.VMEM((1024, 128), f32),
            pltpu.VMEM((256, 1024), bf16),
            pltpu.VMEM((NZ, 128, 256), f32),
            pltpu.VMEM((NZ // 2, NY - 1, 9, 16, 128), bf16),
            pltpu.VMEM((NZ // 2, NY - 1, 9, 16, 128), bf16),
            pltpu.VMEM((NZ - 1, 5, 16, 128), bf16),
            pltpu.VMEM((NZ - 1, 5, 16, 128), bf16),
            pltpu.VMEM((2, NZ, NY, 5, 16, 128), bf16),
            pltpu.VMEM((12, 8, 128), f32),
            sem((3,)), sem((2,)), sem((2,)),
            sem, sem((NZ,)), sem, sem((NZ,)),
            sem, sem((NZ // 2,)), sem, sem((NZ,)),
            sem, sem((NZ,)), sem, sem((NZ,)), sem, sem((NZ,)),
            sem, sem, sem, sem,
        ],
        compiler_params=pltpu.CompilerParams(
            collective_id=0, has_side_effects=True, vmem_limit_bytes=20 * 1024 * 1024
        ),
        cost_estimate=pl.CostEstimate(flops=1 << 31, bytes_accessed=6 << 20, transcendentals=1 << 20),
    )(acts, grad_out, projector)


def update_kernel(
    proj, clip, projector, first_old, second_old, update, first_new, second_new, u_out, f_out, s_out, sem
):
    scale = clip[:1, :]
    scale = jnp.concatenate([scale, scale], axis=1)
    rows = projector[...]
    copies = []
    for i in range(8):
        cols = pl.ds(256 * i, 256)
        clipped = scale * proj[:, cols]
        first = beta_one * first_old[:, cols] + (1.0 - beta_one) * clipped
        second = beta_two * second_old[:, cols] + (1.0 - beta_two) * clipped * clipped
        f_out[:, cols] = first
        s_out[:, cols] = second
        for j, (src, dst) in enumerate(((f_out, first_new), (s_out, second_new))):
            copies.append(pltpu.make_async_copy(src.at[:, cols], dst.at[:, cols], sem.at[i, j]))
            copies[-1].start()
        direction = first * (1.0 / bias_one) / (jnp.sqrt(second * (1.0 / bias_two)) + 1e-08)
        high = direction.astype(bf16)
        low = (direction - high.astype(f32)).astype(bf16)
        moved = jnp.dot(rows, high, preferred_element_type=f32) + jnp.dot(rows, low, preferred_element_type=f32)
        u_out[:, cols] = galore_scale * moved
        copies.append(pltpu.make_async_copy(u_out.at[:, cols], update.at[:, cols], sem.at[i, 2]))
        copies[-1].start()
    for copy in copies:
        copy.wait()


def updated(proj, clip, projector, moment_one, moment_two):
    hbm = pl.BlockSpec(memory_space=pltpu.HBM)
    vmem = pl.BlockSpec(memory_space=pltpu.VMEM)
    return pl.pallas_call(
        update_kernel,
        name="adam_update",
        out_shape=(
            jax.ShapeDtypeStruct((32, 2048), f32),
            jax.ShapeDtypeStruct((256, 2048), f32),
            jax.ShapeDtypeStruct((256, 2048), f32),
        ),
        in_specs=[vmem] * 5,
        out_specs=(hbm, hbm, hbm),
        scratch_shapes=[
            pltpu.VMEM((32, 2048), f32),
            pltpu.VMEM((256, 2048), f32),
            pltpu.VMEM((256, 2048), f32),
            pltpu.SemaphoreType.DMA((8, 3)),
        ],
        compiler_params=pltpu.CompilerParams(vmem_limit_bytes=16 * 1024 * 1024),
        cost_estimate=pl.CostEstimate(flops=1 << 26, bytes_accessed=10 << 20, transcendentals=1 << 20),
    )(proj, clip, projector, moment_one, moment_two)


def on_device(acts, grad_out, projector, moment_one, moment_two):
    entries = float(projector.shape[1] * grad_out.shape[1] * NX)
    acts, grad_out, rows = (pltpu.with_memory_space_constraint(a, pltpu.HBM) for a in (acts, grad_out, projector))
    proj, clip = reduced(acts, grad_out, rows, entries)
    return updated(proj, clip, projector, moment_one, moment_two)


def solution(mesh):
    placed = (P("dp", None), P("dp", "group"), P("dp", None), P(None, "group"), P(None, "group"))
    return jax.shard_map(
        on_device,
        mesh=mesh,
        in_specs=placed,
        out_specs=(P("dp", "group"), P(None, "group"), P(None, "group")),
        check_vma=False,
    )
```

```python
import functools
import math

import jax
import jax.numpy as jnp
from jax import lax
from jax.experimental import pallas as pl
from jax.experimental.pallas import tpu as pltpu
from jax.sharding import PartitionSpec as P

beta_one = 0.9
beta_two = 0.95
bias_one = 1.0 - 0.9**10
bias_two = 1.0 - 0.95**10
galore_scale = 0.25

MESH = pl.DeviceIdType.MESH
NZ, NY, NX = 8, 4, 4
SPAN = 250.0
HALF = 125.0
LN2 = math.log(2.0)
NEAR = (0, 1, 7, 2, 6, 3, 5, 4)
FAR = (4, 3, 5, 2, 6, 1, 7, 0)
f32 = jnp.float32
bf16 = jnp.bfloat16


def tiles_of(block):
    return [block[16 * r : 16 * r + 16, 128 * l : 128 * l + 128] for r in range(2) for l in range(2)]


def scale_of(tiles):
    top = functools.reduce(jnp.maximum, [jnp.abs(t) for t in tiles])
    top = jnp.max(top, axis=0, keepdims=True)
    return (jnp.maximum(top, 1e-30) * 1.01).astype(bf16).astype(f32)


def encode(tiles, scale):
    rate = SPAN / scale
    out = []
    for t in tiles:
        size = jnp.exp2(jnp.abs(t) * rate - HALF)
        out.append(jnp.where(t < 0, -size, size).astype(bf16))
    return out


def decode(codes, scale):
    rate = scale * (1.0 / (SPAN * LN2))
    out = []
    for code in codes:
        code = code.astype(f32)
        size = (jnp.log(jnp.abs(code)) + HALF * LN2) * rate
        out.append(jnp.where(code < 0, -size, size))
    return out


def reduce_kernel(
    entries, acts, grad, p_hbm, proj_out, clip_out,
    p_ref, a_all, g_all, p_all, along, lhs, part,
    yb_send, yb_recv, za_send, za_recv, zb_send, zb_recv, ya_send, ya_recv,
    column, three_all, fourth_all, scale_all, scale_wide, sums,
    load_sem, pair_send, pair_recv, pz_send, pz_recv, py_send, py_recv,
    yb_sent, yb_came, za_sent, za_came, zb_sent, zb_came, ya_sent, ya_came,
    az_sent, az_came, ay_sent, ay_came, by_sent, by_came, bz_sent, bz_came,
    sy_sent, sy_came, sc_sent, sc_came, ac_sent, ac_came, ex_send, ex_recv, ey_send, ey_recv,
):
    dp = lax.axis_index("dp")
    x = lax.axis_index("group")
    c = lax.rem(dp, 2)
    y = lax.rem(lax.div(dp, 2), NY)
    z = lax.div(dp, 2 * NY)

    def at(zz, yy, cc, xx):
        return ((zz * NY + yy) * 2 + cc, xx)

    def zoff(d):
        return lax.rem(z + d, NZ)

    def yoff(d):
        return lax.rem(y + d, NY)

    def xoff(d):
        return lax.rem(x + d, NX)

    def remote(src, dst, send, recv, device):
        return pltpu.make_async_remote_copy(
            src_ref=src, dst_ref=dst, send_sem=send, recv_sem=recv, device_id=device, device_id_type=MESH
        )

    me = at(z, y, c, x)
    sibling = at(z, y, 1 - c, x)

    def arrived(ref, recv):
        remote(ref, ref, pz_send, recv, me).wait_recv()

    def sent(ref, send):
        remote(ref, ref, send, pz_recv.at[0], me).wait_send()

    loads = [
        pltpu.make_async_copy(p_hbm, p_ref, load_sem.at[2]),
        pltpu.make_async_copy(acts, a_all.at[pl.ds(0, 512)], load_sem.at[0]),
        pltpu.make_async_copy(grad, g_all.at[pl.ds(0, 512)], load_sem.at[1]),
    ]
    for copy in loads:
        copy.start()

    barrier = pltpu.get_barrier_semaphore()
    peers = [at(zoff(d), y, cc, x) for d in NEAR[:0:-1] for cc in range(2)]
    peers += [at(z, yoff(d), cc, x) for d in range(1, NY) for cc in range(2)] + [sibling]
    peers += [at(z, y, c, xoff(d)) for d in range(1, NX)]
    for peer in peers:
        pl.semaphore_signal(barrier, inc=1, device_id=peer, device_id_type=MESH)
    loads[0].wait()
    pl.semaphore_wait(barrier, len(peers))

    mine = pl.ds(pl.multiple_of((z * NY + y) * 64 + c * 32, 32), 32)
    for cc in range(2):

        @pl.when(c != cc)
        def _():
            remote(p_ref.at[:, pl.ds(cc * 128, 128)], p_all.at[mine], pz_send, pz_recv.at[0], sibling).start()

        @pl.when(c == cc)
        def _():
            p_all[mine, :] = p_ref[:, cc * 128 : cc * 128 + 128]

    for d in NEAR[:0:-1]:
        for cc in range(2):
            src = p_ref.at[:, pl.ds(cc * 128, 128)]
            remote(src, p_all.at[mine], pz_send, pz_recv.at[d], at(zoff(d), y, cc, x)).start()

    pair = [
        remote(acts, a_all.at[pl.ds(512, 512)], pair_send.at[0], pair_recv.at[0], sibling),
        remote(grad, g_all.at[pl.ds(512, 512)], pair_send.at[1], pair_recv.at[1], sibling),
    ]
    for copy in pair:
        copy.start()

    def p_rows(zz, yy, n=64):
        return pl.ds(pl.multiple_of((zz * NY + yy) * 64, 64), n)

    def p_forward(d):
        chunk = p_all.at[p_rows(zoff(NZ - d), y)]
        arrived(chunk if d else p_all.at[pl.ds(0, 32)], pz_recv.at[d])
        for dy in (2, 1, 3):
            remote(chunk, chunk, py_send, py_recv.at[d], at(z, yoff(dy), c, x)).start()

    def p_use(d, first):
        zz = zoff(NZ - d)
        arrived(p_all.at[pl.ds(0, 192)], py_recv.at[d])
        if first:
            loads[1].wait()
            pair[0].wait_recv()
        cols = pl.ds(pl.multiple_of(zz * 256, 256), 256)
        term = jnp.dot(a_all[:, cols], p_all[p_rows(zz, 0, 256), :], preferred_element_type=f32)
        if first:
            along[...] = term
        else:
            along[...] += term

    lag = 4
    for k in range(NZ + lag):
        if k < NZ:
            p_forward(NEAR[k])
        if k >= lag:
            p_use(NEAR[k - lag], k == lag)

    turned = along[...].T
    high = turned.astype(bf16)
    lhs[pl.ds(0, 128), :] = high
    lhs[pl.ds(128, 128), :] = (turned - high.astype(f32)).astype(bf16)
    loads[2].wait()
    pair[1].wait_recv()

    row = lax.broadcasted_iota(jnp.int32, (16, 128), 0)

    def block_rows(dy, rh, n):
        return pl.ds(pl.multiple_of(yoff(dy) * 32 + 16 * rh, 16), n)

    def three_tiles(k, dy):
        top = part[k, block_rows(dy, 0, 16), :]
        return [top[:, :128], top[:, 128:], part[k, block_rows(dy, 1, 16), :128]]

    def fourth_tile(k, dy):
        return part[k, block_rows(dy, 1, 16), 128:]

    for k, d in enumerate(FAR):
        cols = pl.ds(pl.multiple_of(zoff(d) * 256, 256), 256)
        both = jnp.dot(lhs[...], g_all[:, cols], preferred_element_type=f32)
        part[k] = both[:128] + both[128:]
        if d:
            message = za_send.at[d - 1]
            scales = jnp.zeros((16, 128), f32)
            for dy in range(NY):
                tile = fourth_tile(k, dy)
                scale = scale_of([tile])
                message[dy] = encode([tile], scale)[0]
                scales = jnp.where(row // 4 == dy, scale, scales)
            message[4] = scales.astype(bf16)
            remote(message, za_recv.at[d - 1], za_sent, za_came.at[d], at(zoff(d), y, c, x)).start()
        if k % 2 == 0:
            continue
        for dy in (2, 1, 3):
            message = yb_send.at[k // 2, dy - 1]
            scales = []
            for j in range(2):
                tiles = three_tiles(k - 1 + j, dy)
                scales.append(scale_of(tiles))
                for i, code in enumerate(encode(tiles, scales[j])):
                    message[3 * j + i] = code
            message[6] = jnp.where(row < 8, scales[0], scales[1]).astype(bf16)
            remote(
                message, yb_recv.at[k // 2, dy - 1], yb_sent, yb_came.at[k // 2], at(z, yoff(dy), c, x)
            ).start()

    sent(p_all.at[pl.ds(0, 480)], pz_send)
    sent(p_all.at[pl.ds(0, 1536)], py_send)
    for copy in pair:
        copy.wait_send()

    def add(total, codes, scale):
        return [a + b for a, b in zip(total, decode(codes, scale))]

    def second_b(k, d):
        if k % 2 == 0:
            arrived(yb_recv.at[k // 2], yb_came.at[k // 2])
        total = three_tiles(k, 0)
        for i in range(NY - 1):
            message = yb_recv.at[k // 2, i]
            scale = message[6][8 * (k % 2) : 8 * (k % 2) + 1].astype(f32)
            total = add(total, [message[3 * (k % 2) + j] for j in range(3)], scale)
        if d:
            message = zb_send.at[d - 1]
            scale = scale_of(total)
            for i, code in enumerate(encode(total, scale)):
                message[i] = code
            message[3] = jnp.broadcast_to(scale, (16, 128)).astype(bf16)
            remote(message, zb_recv.at[d - 1], zb_sent, zb_came.at[d], at(zoff(d), y, c, x)).start()
        return total

    for k in range(4):
        second_b(k, FAR[k])
    fourths = [fourth_tile(NZ - 1, dy) for dy in range(NY)]
    for d in NEAR[1:]:
        message = za_recv.at[d - 1]
        arrived(message, za_came.at[d])
        scales = message[4].astype(f32)
        for dy in range(NY):
            fourths[dy] = add([fourths[dy]], [message[dy]], scales[4 * dy : 4 * dy + 1])[0]
    for dy in (2, 1, 3):
        message = ya_send.at[dy - 1]
        scale = scale_of([fourths[dy]])
        message[0] = encode([fourths[dy]], scale)[0]
        message[1] = jnp.broadcast_to(scale, (16, 128)).astype(bf16)
        remote(message, ya_recv.at[dy - 1], ya_sent, ya_came, at(z, yoff(dy), c, x)).start()
    for k in range(4, NZ):
        total = second_b(k, FAR[k])
    fourth = [fourths[0]]
    arrived(ya_recv, ya_came)
    for dy in range(1, NY):
        message = ya_recv.at[dy - 1]
        fourth = add(fourth, [message[0]], message[1][:1].astype(f32))
    sent(yb_send, yb_sent)
    sent(za_send, za_sent)
    for d in NEAR[1:]:
        message = zb_recv.at[d - 1]
        arrived(message, zb_came.at[d])
        total = add(total, [message[j] for j in range(3)], message[3][:1].astype(f32))
    total = total + fourth

    scale = scale_of(total)
    codes = encode(total, scale)
    fourth_all[c, z, y] = codes[3]
    for dy in (2, 1, 3):
        block = fourth_all.at[c, z, y]
        remote(block, block, by_sent, by_came, at(z, yoff(dy), c, x)).start()
    energy = jnp.sum(functools.reduce(jnp.add, [t * t for t in total]), axis=0, keepdims=True)
    e_high = energy.astype(bf16).astype(f32)
    e_mid = (energy - e_high).astype(bf16).astype(f32)
    e_low = energy - e_high - e_mid
    last = jnp.where(row < 8, scale, 0.0)
    for i, part_of in enumerate((e_high, e_mid, e_low)):
        last = jnp.where(row == 8 + i, part_of, last)
    packet = column.at[z]
    for i in range(3):
        packet[i] = codes[i]
    packet[3] = last.astype(bf16)
    for d in NEAR[:0:-1]:
        remote(packet, packet, az_sent, az_came.at[d], at(zoff(d), y, c, x)).start()

    def out_forward(d):
        zz = zoff(NZ - d)
        if d:
            arrived(column.at[zz], az_came.at[d])
        block = column.at[zz, pl.ds(0, 3)]
        for dy in (2, 1, 3):
            remote(block, three_all.at[c, zz, y], ay_sent, ay_came.at[d], at(z, yoff(dy), c, x)).start()
        three_all[c, zz, y] = column[zz, pl.ds(0, 3)]

    def out_share(d):
        zz = zoff(NZ - d)
        arrived(three_all.at[c, zz, pl.ds(0, 3)], ay_came.at[d])
        if d:
            arrived(fourth_all.at[c, zz], bz_came.at[d])
        for ref in (three_all, fourth_all):
            remote(ref.at[c, zz], ref.at[c, zz], ac_sent, ac_came.at[d], sibling).start()

    for k in range(NZ):
        out_forward(NEAR[k])
        if k == 2:
            arrived(fourth_all.at[c, z, pl.ds(0, 3)], by_came)
            for d in NEAR[:0:-1]:
                block = fourth_all.at[c, z]
                remote(block, block, bz_sent, bz_came.at[d], at(zoff(d), y, c, x)).start()

    tiles = [column[zz, 3].astype(f32) for zz in range(NZ)]
    scales = functools.reduce(lambda a, b: jnp.where(row == b, tiles[b], a), range(1, NZ), tiles[0])
    scale_all[c, y] = scales.astype(bf16)
    for dy in (2, 1, 3):
        block = scale_all.at[c, y]
        remote(block, block, sy_sent, sy_came, at(z, yoff(dy), c, x)).start()
    tile = functools.reduce(jnp.add, tiles)
    sums[0] = jnp.where(row[:8] < 3, tile[8:], 0.0)
    for d in (2, 1, 3):
        remote(sums.at[0], sums.at[d], ex_send, ex_recv, at(z, y, c, xoff(d))).start()
    sent(zb_send, zb_sent)
    sent(ya_send, ya_sent)

    def widen(cc):
        scale_wide[cc] = scale_all[cc].astype(f32)

    def unpack(cc, zz):
        for yy in range(NY):
            codes = [three_all[cc, zz, yy, j] for j in range(3)] + [fourth_all[cc, zz, yy]]
            for i, t in enumerate(decode(codes, scale_wide[cc, yy, pl.ds(zz, 1), :])):
                rows = pl.ds(pl.multiple_of(cc * 128 + yy * 32 + (i // 2) * 16, 16), 16)
                cols = pl.ds(pl.multiple_of(zz * 256 + (i % 2) * 128, 128), 128)
                proj_out[rows, cols] = t

    for k in range(3):
        out_share(NEAR[k])
    arrived(sums.at[pl.ds(0, 3)], ex_recv)
    sums[4] = sums[0] + sums[1] + sums[2] + sums[3]
    slot = 5
    for dy in (2, 1, 3, 0):
        for dc in (1, 0):
            if dy or dc:
                cc = lax.rem(c + dc, 2)
                remote(sums.at[4], sums.at[slot], ey_send, ey_recv, at(z, yoff(dy), cc, x)).start()
                slot += 1
    arrived(scale_all.at[c, pl.ds(0, 3)], sy_came)
    remote(scale_all.at[c], scale_all.at[c], sc_sent, sc_came, sibling).start()
    widen(c)
    for k in range(3, NZ):
        out_share(NEAR[k])
        unpack(c, zoff(NZ - NEAR[k - 3]))
    for k in range(NZ - 3, NZ):
        unpack(c, zoff(NZ - NEAR[k]))
    arrived(scale_all.at[1 - c], sc_came)
    widen(1 - c)
    for k, d in enumerate(NEAR):
        zz = zoff(NZ - d)
        arrived(fourth_all.at[0, pl.ds(0, 4)], ac_came.at[d])
        unpack(1 - c, zz)
        if k == 3:
            arrived(sums.at[pl.ds(0, 7)], ey_recv)
            energy = functools.reduce(jnp.add, [sums[i] for i in range(4, 12)])
            mean = jnp.full((8, 128), jnp.sum(energy) / entries + 1e-06, f32)
            clip_out[...] = jnp.minimum(1.0, 1.0 / jnp.sqrt(mean))

    sent(column.at[pl.ds(0, 7)], az_sent)
    sent(three_all.at[0, pl.ds(0, 6)], ay_sent)
    sent(fourth_all.at[0, 0, pl.ds(0, 3)], by_sent)
    sent(fourth_all.at[0, pl.ds(0, 7)], bz_sent)
    sent(scale_all.at[0, pl.ds(0, 3)], sy_sent)
    sent(scale_all.at[0], sc_sent)
    sent(fourth_all.at[0], ac_sent)
    sent(three_all.at[0], ac_sent)
    sent(sums.at[pl.ds(0, 3)], ex_send)
    sent(sums.at[pl.ds(0, 7)], ey_send)


def reduced(acts, grad_out, projector, entries):
    sem = pltpu.SemaphoreType.DMA
    hbm = pl.BlockSpec(memory_space=pltpu.HBM)
    vmem = pl.BlockSpec(memory_space=pltpu.VMEM)
    return pl.pallas_call(
        functools.partial(reduce_kernel, entries),
        name="projected_gradient",
        out_shape=(jax.ShapeDtypeStruct((256, 2048), f32), jax.ShapeDtypeStruct((8, 128), f32)),
        in_specs=[hbm, hbm, hbm],
        out_specs=(vmem, vmem),
        scratch_shapes=[
            pltpu.VMEM((32, 256), bf16),
            pltpu.VMEM((1024, 2048), bf16),
            pltpu.VMEM((1024, 2048), bf16),
            pltpu.VMEM((2048, 128), bf16),
            pltpu.VMEM((1024, 128), f32),
            pltpu.VMEM((256, 1024), bf16),
            pltpu.VMEM((NZ, 128, 256), f32),
            pltpu.VMEM((NZ // 2, NY - 1, 7, 16, 128), bf16),
            pltpu.VMEM((NZ // 2, NY - 1, 7, 16, 128), bf16),
            pltpu.VMEM((NZ - 1, 5, 16, 128), bf16),
            pltpu.VMEM((NZ - 1, 5, 16, 128), bf16),
            pltpu.VMEM((NZ - 1, 4, 16, 128), bf16),
            pltpu.VMEM((NZ - 1, 4, 16, 128), bf16),
            pltpu.VMEM((NY - 1, 2, 16, 128), bf16),
            pltpu.VMEM((NY - 1, 2, 16, 128), bf16),
            pltpu.VMEM((NZ, 4, 16, 128), bf16),
            pltpu.VMEM((2, NZ, NY, 3, 16, 128), bf16),
            pltpu.VMEM((2, NZ, NY, 16, 128), bf16),
            pltpu.VMEM((2, NY, 16, 128), bf16),
            pltpu.VMEM((2, NY, 16, 128), f32),
            pltpu.VMEM((12, 8, 128), f32),
            sem((3,)), sem((2,)), sem((2,)),
            sem, sem((NZ,)), sem, sem((NZ,)),
            sem, sem((NZ // 2,)), sem, sem((NZ,)), sem, sem((NZ,)), sem, sem,
            sem, sem((NZ,)), sem, sem((NZ,)), sem, sem, sem, sem((NZ,)),
            sem, sem, sem, sem, sem, sem((NZ,)), sem, sem, sem, sem,
        ],
        compiler_params=pltpu.CompilerParams(
            collective_id=0, has_side_effects=True, vmem_limit_bytes=20 * 1024 * 1024
        ),
        cost_estimate=pl.CostEstimate(flops=1 << 31, bytes_accessed=6 << 20, transcendentals=1 << 20),
    )(acts, grad_out, projector)


def update_kernel(
    proj, clip, projector, first_old, second_old, update, first_new, second_new, u_out, f_out, s_out, sem
):
    scale = clip[:1, :]
    scale = jnp.concatenate([scale, scale], axis=1)
    rows = projector[...]
    copies = []

    def start(src, dst, i, j):
        cols = pl.ds(256 * i, 256)
        copies.append(pltpu.make_async_copy(src.at[:, cols], dst.at[:, cols], sem.at[i, j]))
        copies[-1].start()

    def project(i, high, low):
        moved = jnp.dot(rows, high, preferred_element_type=f32) + jnp.dot(rows, low, preferred_element_type=f32)
        u_out[:, pl.ds(256 * i, 256)] = galore_scale * moved

    waiting = None
    for i in range(8):
        cols = pl.ds(256 * i, 256)
        if i:
            project(i - 1, *waiting)
        clipped = scale * proj[:, cols]
        first = beta_one * first_old[:, cols] + (1.0 - beta_one) * clipped
        second = beta_two * second_old[:, cols] + (1.0 - beta_two) * clipped * clipped
        f_out[:, cols] = first
        s_out[:, cols] = second
        square = second * (1.0 / bias_two)
        direction = first * (1.0 / bias_one) / (square * lax.rsqrt(square) + 1e-08)
        high = direction.astype(bf16)
        waiting = (high, (direction - high.astype(f32)).astype(bf16))
        start(f_out, first_new, i, 0)
        start(s_out, second_new, i, 1)
        if i:
            start(u_out, update, i - 1, 2)
    project(7, *waiting)
    start(u_out, update, 7, 2)
    for copy in copies:
        copy.wait()


def updated(proj, clip, projector, moment_one, moment_two):
    hbm = pl.BlockSpec(memory_space=pltpu.HBM)
    vmem = pl.BlockSpec(memory_space=pltpu.VMEM)
    return pl.pallas_call(
        update_kernel,
        name="adam_update",
        out_shape=(
            jax.ShapeDtypeStruct((32, 2048), f32),
            jax.ShapeDtypeStruct((256, 2048), f32),
            jax.ShapeDtypeStruct((256, 2048), f32),
        ),
        in_specs=[vmem] * 5,
        out_specs=(hbm, hbm, hbm),
        scratch_shapes=[
            pltpu.VMEM((32, 2048), f32),
            pltpu.VMEM((256, 2048), f32),
            pltpu.VMEM((256, 2048), f32),
            pltpu.SemaphoreType.DMA((8, 3)),
        ],
        compiler_params=pltpu.CompilerParams(vmem_limit_bytes=16 * 1024 * 1024),
        cost_estimate=pl.CostEstimate(flops=1 << 26, bytes_accessed=10 << 20, transcendentals=1 << 20),
    )(proj, clip, projector, moment_one, moment_two)


def on_device(acts, grad_out, projector, moment_one, moment_two):
    entries = float(projector.shape[1] * grad_out.shape[1] * NX)
    acts, grad_out, rows = (pltpu.with_memory_space_constraint(a, pltpu.HBM) for a in (acts, grad_out, projector))
    proj, clip = reduced(acts, grad_out, rows, entries)
    return updated(proj, clip, projector, moment_one, moment_two)


def solution(mesh):
    placed = (P("dp", None), P("dp", "group"), P("dp", None), P(None, "group"), P(None, "group"))
    return jax.shard_map(
        on_device,
        mesh=mesh,
        in_specs=placed,
        out_specs=(P("dp", "group"), P(None, "group"), P(None, "group")),
        check_vma=False,
    )
```

```python
import functools
import math

import jax
import jax.numpy as jnp
from jax import lax
from jax.experimental import pallas as pl
from jax.experimental.pallas import tpu as pltpu
from jax.sharding import PartitionSpec as P

beta_one = 0.9
beta_two = 0.95
bias_one = 1.0 - 0.9**10
bias_two = 1.0 - 0.95**10
galore_scale = 0.25

MESH = pl.DeviceIdType.MESH
NZ, NY, NX = 8, 4, 4
SPAN = 250.0
HALF = 125.0
LN2 = math.log(2.0)
NEAR = (0, 1, 7, 2, 6, 3, 5, 4)
FAR = (4, 3, 5, 2, 6, 1, 7, 0)
f32 = jnp.float32
bf16 = jnp.bfloat16


def tiles_of(block):
    return [block[16 * r : 16 * r + 16, 128 * l : 128 * l + 128] for r in range(2) for l in range(2)]


def scale_of(tiles):
    top = functools.reduce(jnp.maximum, [jnp.abs(t) for t in tiles])
    top = jnp.max(top, axis=0, keepdims=True)
    return (jnp.maximum(top, 1e-30) * 1.01).astype(bf16).astype(f32)


def encode(tiles, scale):
    rate = SPAN / scale
    out = []
    for t in tiles:
        size = jnp.exp2(jnp.abs(t) * rate - HALF)
        out.append(jnp.where(t < 0, -size, size).astype(bf16))
    return out


def decode(codes, scale):
    rate = scale * (1.0 / (SPAN * LN2))
    out = []
    for code in codes:
        code = code.astype(f32)
        size = (jnp.log(jnp.abs(code)) + HALF * LN2) * rate
        out.append(jnp.where(code < 0, -size, size))
    return out


def reduce_kernel(
    entries, acts, grad, p_hbm, proj_out, clip_out,
    p_ref, a_all, g_all, p_all, along, lhs, part,
    yb_send, yb_recv, zb_send, zb_recv, column, blocks, scale_all, scale_wide, sums,
    load_sem, pair_send, pair_recv, pz_send, pz_recv, py_send, py_recv,
    yb_sent, yb_came, zb_sent, zb_came, az_sent, az_came, ay_sent, ay_came,
    sy_sent, sy_came, sc_sent, sc_came, ac_sent, ac_came,
    ex_send, ex_recv, ez_send, ez_recv, ey_send, ey_recv,
):
    dp = lax.axis_index("dp")
    x = lax.axis_index("group")
    c = lax.rem(dp, 2)
    y = lax.rem(lax.div(dp, 2), NY)
    z = lax.div(dp, 2 * NY)

    def at(zz, yy, cc, xx):
        return ((zz * NY + yy) * 2 + cc, xx)

    def zoff(d):
        return lax.rem(z + d, NZ)

    def yoff(d):
        return lax.rem(y + d, NY)

    def xoff(d):
        return lax.rem(x + d, NX)

    def remote(src, dst, send, recv, device):
        return pltpu.make_async_remote_copy(
            src_ref=src, dst_ref=dst, send_sem=send, recv_sem=recv, device_id=device, device_id_type=MESH
        )

    me = at(z, y, c, x)
    sibling = at(z, y, 1 - c, x)

    def arrived(ref, recv):
        remote(ref, ref, pz_send, recv, me).wait_recv()

    def sent(ref, send):
        remote(ref, ref, send, pz_recv.at[0], me).wait_send()

    loads = [
        pltpu.make_async_copy(p_hbm, p_ref, load_sem.at[2]),
        pltpu.make_async_copy(acts, a_all.at[pl.ds(0, 512)], load_sem.at[0]),
        pltpu.make_async_copy(grad, g_all.at[pl.ds(0, 512)], load_sem.at[1]),
    ]
    for copy in loads:
        copy.start()

    barrier = pltpu.get_barrier_semaphore()
    peers = [at(zoff(d), y, cc, x) for d in NEAR[:0:-1] for cc in range(2)]
    peers += [at(z, yoff(d), cc, x) for d in range(1, NY) for cc in range(2)] + [sibling]
    peers += [at(z, y, c, xoff(d)) for d in range(1, NX)]
    for peer in peers:
        pl.semaphore_signal(barrier, inc=1, device_id=peer, device_id_type=MESH)
    loads[0].wait()
    pl.semaphore_wait(barrier, len(peers))

    mine = pl.ds(pl.multiple_of((z * NY + y) * 64 + c * 32, 32), 32)
    for cc in range(2):

        @pl.when(c != cc)
        def _():
            remote(p_ref.at[:, pl.ds(cc * 128, 128)], p_all.at[mine], pz_send, pz_recv.at[0], sibling).start()

        @pl.when(c == cc)
        def _():
            p_all[mine, :] = p_ref[:, cc * 128 : cc * 128 + 128]

    for d in NEAR[1:]:
        for cc in range(2):
            src = p_ref.at[:, pl.ds(cc * 128, 128)]
            remote(src, p_all.at[mine], pz_send, pz_recv.at[d], at(zoff(d), y, cc, x)).start()

    pair = [
        remote(acts, a_all.at[pl.ds(512, 512)], pair_send.at[0], pair_recv.at[0], sibling),
        remote(grad, g_all.at[pl.ds(512, 512)], pair_send.at[1], pair_recv.at[1], sibling),
    ]
    for copy in pair:
        copy.start()

    def p_rows(zz, yy, n=64):
        return pl.ds(pl.multiple_of((zz * NY + yy) * 64, 64), n)

    def p_forward(d):
        chunk = p_all.at[p_rows(zoff(NZ - d), y)]
        arrived(chunk if d else p_all.at[pl.ds(0, 32)], pz_recv.at[d])
        for dy in (2, 1, 3):
            remote(chunk, chunk, py_send, py_recv.at[d], at(z, yoff(dy), c, x)).start()

    def p_use(d, first):
        zz = zoff(NZ - d)
        arrived(p_all.at[pl.ds(0, 192)], py_recv.at[d])
        if first:
            loads[1].wait()
            pair[0].wait_recv()
        cols = pl.ds(pl.multiple_of(zz * 256, 256), 256)
        term = jnp.dot(a_all[:, cols], p_all[p_rows(zz, 0, 256), :], preferred_element_type=f32)
        if first:
            along[...] = term
        else:
            along[...] += term

    lag = 4
    for k in range(NZ + lag):
        if k < NZ:
            p_forward(NEAR[k])
        if k >= lag:
            p_use(NEAR[k - lag], k == lag)

    turned = along[...].T
    high = turned.astype(bf16)
    lhs[pl.ds(0, 128), :] = high
    lhs[pl.ds(128, 128), :] = (turned - high.astype(f32)).astype(bf16)
    loads[2].wait()
    pair[1].wait_recv()

    row = lax.broadcasted_iota(jnp.int32, (16, 128), 0)

    def four_tiles(k, dy):
        return tiles_of(part[k, pl.ds(pl.multiple_of(yoff(dy) * 32, 32), 32), :])

    def multiply(p):
        for k in (2 * p, 2 * p + 1):
            cols = pl.ds(pl.multiple_of(zoff(FAR[k]) * 256, 256), 256)
            both = jnp.dot(lhs[...], g_all[:, cols], preferred_element_type=f32)
            part[k] = both[:128] + both[128:]

    def first_b(p, dy):
        message = yb_send.at[p, dy - 1]
        scales = []
        for j in range(2):
            tiles = four_tiles(2 * p + j, dy)
            scales.append(scale_of(tiles))
            for i, code in enumerate(encode(tiles, scales[j])):
                message[4 * j + i] = code
        message[8] = jnp.where(row < 8, scales[0], scales[1]).astype(bf16)

    multiply(0)
    for p in range(NZ // 2):
        if p < NZ // 2 - 1:
            multiply(p + 1)
        for dy in (2, 1, 3):
            first_b(p, dy)
        for dy in (2, 1, 3):
            remote(
                yb_send.at[p, dy - 1], yb_recv.at[p, dy - 1], yb_sent, yb_came.at[p], at(z, yoff(dy), c, x)
            ).start()

    sent(p_all.at[pl.ds(0, 480)], pz_send)
    sent(p_all.at[pl.ds(0, 1536)], py_send)
    for copy in pair:
        copy.wait_send()

    def add(total, codes, scale):
        return [a + b for a, b in zip(total, decode(codes, scale))]

    def second_b(p):
        arrived(yb_recv.at[p], yb_came.at[p])
        for j, d in enumerate((FAR[2 * p], FAR[2 * p + 1])):
            total = four_tiles(2 * p + j, 0)
            for i in range(NY - 1):
                message = yb_recv.at[p, i]
                scale = message[8][8 * j : 8 * j + 1].astype(f32)
                total = add(total, [message[4 * j + t] for t in range(4)], scale)
            if d:
                message = zb_send.at[d - 1]
                scale = scale_of(total)
                for i, code in enumerate(encode(total, scale)):
                    message[i] = code
                message[4] = jnp.broadcast_to(scale, (16, 128)).astype(bf16)
        for d in (FAR[2 * p], FAR[2 * p + 1]):
            if d:
                remote(
                    zb_send.at[d - 1], zb_recv.at[d - 1], zb_sent, zb_came.at[d], at(zoff(d), y, c, x)
                ).start()
        return total

    for p in range(NZ // 2):
        total = second_b(p)
    sent(yb_send, yb_sent)
    for d in NEAR[1:]:
        message = zb_recv.at[d - 1]
        arrived(message, zb_came.at[d])
        total = add(total, [message[j] for j in range(4)], message[4][:1].astype(f32))

    square = functools.reduce(jnp.add, [t * t for t in total])
    sums[0] = square[:8] + square[8:]
    scale = scale_of(total)
    packet = column.at[z]
    for i, code in enumerate(encode(total, scale)):
        packet[i] = code
    packet[4] = jnp.broadcast_to(scale, (16, 128)).astype(bf16)
    for d in (2, 1, 3):
        remote(sums.at[0], sums.at[d], ex_send, ex_recv, at(z, y, c, xoff(d))).start()
    for d in NEAR[1:]:
        remote(packet, packet, az_sent, az_came.at[d], at(zoff(d), y, c, x)).start()

    def out_forward(d):
        zz = zoff(NZ - d)
        if d:
            arrived(column.at[zz], az_came.at[d])
        block = column.at[zz, pl.ds(0, 4)]
        for dy in (2, 1, 3):
            remote(block, blocks.at[c, zz, y], ay_sent, ay_came.at[d], at(z, yoff(dy), c, x)).start()
        blocks[c, zz, y] = column[zz, pl.ds(0, 4)]

    def out_share(d):
        block = blocks.at[c, zoff(NZ - d)]
        arrived(blocks.at[c, zoff(NZ - d), pl.ds(0, 3)], ay_came.at[d])
        remote(block, block, ac_sent, ac_came.at[d], sibling).start()

    for k in range(NZ):
        out_forward(NEAR[k])
        if k == 2:
            arrived(sums.at[pl.ds(0, 3)], ex_recv)
            sums[4] = sums[0] + sums[1] + sums[2] + sums[3]
            for d in NEAR[:0:-1]:
                remote(sums.at[4], sums.at[4 + d], ez_send, ez_recv, at(zoff(d), y, c, x)).start()

    tiles = [column[zz, 4] for zz in range(NZ)]
    scale_all[c, y] = functools.reduce(lambda a, b: jnp.where(row == b, tiles[b], a), range(1, NZ), tiles[0])
    for dy in (2, 1, 3):
        block = scale_all.at[c, y]
        remote(block, block, sy_sent, sy_came, at(z, yoff(dy), c, x)).start()
    arrived(sums.at[pl.ds(0, 7)], ez_recv)
    sums[12] = functools.reduce(jnp.add, [sums[i] for i in range(4, 12)])
    slot = 13
    for dy in (2, 1, 3, 0):
        for dc in (1, 0):
            if dy or dc:
                cc = lax.rem(c + dc, 2)
                remote(sums.at[12], sums.at[slot], ey_send, ey_recv, at(z, yoff(dy), cc, x)).start()
                slot += 1
    sent(zb_send, zb_sent)

    def widen(cc):
        scale_wide[cc] = scale_all[cc].astype(f32)

    def unpack(cc, zz):
        for yy in range(NY):
            codes = [blocks[cc, zz, yy, j] for j in range(4)]
            for i, t in enumerate(decode(codes, scale_wide[cc, yy, pl.ds(zz, 1), :])):
                rows = pl.ds(pl.multiple_of(cc * 128 + yy * 32 + (i // 2) * 16, 16), 16)
                cols = pl.ds(pl.multiple_of(zz * 256 + (i % 2) * 128, 128), 128)
                proj_out[rows, cols] = t

    def near(k):
        return lax.rem(jnp.where(lax.rem(k, 2) == 1, lax.div(k + 1, 2), NZ - lax.div(k, 2)), NZ)

    def unpack_own(k, carry):
        unpack(c, zoff(NZ - near(k)))
        return carry

    def unpack_theirs(k, carry):
        d = near(k)
        zz = zoff(NZ - d)
        arrived(blocks.at[1 - c, zz], ac_came.at[d])
        unpack(1 - c, zz)
        return carry

    for k in range(NZ - 2):
        out_share(NEAR[k])
    arrived(scale_all.at[c, pl.ds(0, 3)], sy_came)
    remote(scale_all.at[c], scale_all.at[c], sc_sent, sc_came, sibling).start()
    widen(c)
    lax.fori_loop(0, NZ // 2, unpack_own, 0)
    for k in range(NZ - 2, NZ):
        out_share(NEAR[k])
    lax.fori_loop(NZ // 2, NZ, unpack_own, 0)
    arrived(scale_all.at[1 - c], sc_came)
    widen(1 - c)
    lax.fori_loop(0, NZ - 2, unpack_theirs, 0)
    arrived(sums.at[pl.ds(0, 7)], ey_recv)
    energy = functools.reduce(jnp.add, [sums[i] for i in range(12, 20)])
    mean = jnp.full((8, 128), jnp.sum(energy) / entries + 1e-06, f32)
    clip_out[...] = jnp.minimum(1.0, 1.0 / jnp.sqrt(mean))
    lax.fori_loop(NZ - 2, NZ, unpack_theirs, 0)

    sent(column.at[pl.ds(0, 7)], az_sent)
    sent(blocks.at[0, pl.ds(0, 6)], ay_sent)
    sent(scale_all.at[0, pl.ds(0, 3)], sy_sent)
    sent(scale_all.at[0], sc_sent)
    sent(blocks.at[0], ac_sent)
    sent(sums.at[pl.ds(0, 3)], ex_send)
    sent(sums.at[pl.ds(0, 7)], ez_send)
    sent(sums.at[pl.ds(0, 7)], ey_send)


def reduced(acts, grad_out, projector, entries):
    sem = pltpu.SemaphoreType.DMA
    hbm = pl.BlockSpec(memory_space=pltpu.HBM)
    vmem = pl.BlockSpec(memory_space=pltpu.VMEM)
    return pl.pallas_call(
        functools.partial(reduce_kernel, entries),
        name="projected_gradient",
        out_shape=(jax.ShapeDtypeStruct((256, 2048), f32), jax.ShapeDtypeStruct((8, 128), f32)),
        in_specs=[hbm, hbm, hbm],
        out_specs=(vmem, vmem),
        scratch_shapes=[
            pltpu.VMEM((32, 256), bf16),
            pltpu.VMEM((1024, 2048), bf16),
            pltpu.VMEM((1024, 2048), bf16),
            pltpu.VMEM((2048, 128), bf16),
            pltpu.VMEM((1024, 128), f32),
            pltpu.VMEM((256, 1024), bf16),
            pltpu.VMEM((NZ, 128, 256), f32),
            pltpu.VMEM((NZ // 2, NY - 1, 9, 16, 128), bf16),
            pltpu.VMEM((NZ // 2, NY - 1, 9, 16, 128), bf16),
            pltpu.VMEM((NZ - 1, 5, 16, 128), bf16),
            pltpu.VMEM((NZ - 1, 5, 16, 128), bf16),
            pltpu.VMEM((NZ, 5, 16, 128), bf16),
            pltpu.VMEM((2, NZ, NY, 4, 16, 128), bf16),
            pltpu.VMEM((2, NY, 16, 128), bf16),
            pltpu.VMEM((2, NY, 16, 128), f32),
            pltpu.VMEM((20, 8, 128), f32),
            sem((3,)), sem((2,)), sem((2,)), sem, sem((NZ,)), sem, sem((NZ,)),
            sem, sem((NZ // 2,)), sem, sem((NZ,)), sem, sem((NZ,)), sem, sem((NZ,)),
            sem, sem, sem, sem, sem, sem((NZ,)),
            sem, sem, sem, sem, sem, sem,
        ],
        compiler_params=pltpu.CompilerParams(
            collective_id=0, has_side_effects=True, vmem_limit_bytes=20 * 1024 * 1024
        ),
        cost_estimate=pl.CostEstimate(flops=1 << 31, bytes_accessed=6 << 20, transcendentals=1 << 20),
    )(acts, grad_out, projector)


def update_kernel(
    proj, clip, projector, first_old, second_old, update, first_new, second_new, u_out, f_out, s_out, sem
):
    scale = clip[:1, :]
    scale = jnp.concatenate([scale, scale], axis=1)
    rows = projector[...]
    copies = []

    def start(src, dst, i, j):
        cols = pl.ds(256 * i, 256)
        copies.append(pltpu.make_async_copy(src.at[:, cols], dst.at[:, cols], sem.at[i, j]))
        copies[-1].start()

    def project(i, high, low):
        moved = jnp.dot(rows, high, preferred_element_type=f32) + jnp.dot(rows, low, preferred_element_type=f32)
        u_out[:, pl.ds(256 * i, 256)] = galore_scale * moved

    waiting = None
    for i in range(8):
        cols = pl.ds(256 * i, 256)
        if i:
            project(i - 1, *waiting)
        clipped = scale * proj[:, cols]
        first = beta_one * first_old[:, cols] + (1.0 - beta_one) * clipped
        second = beta_two * second_old[:, cols] + (1.0 - beta_two) * clipped * clipped
        f_out[:, cols] = first
        s_out[:, cols] = second
        square = second * (1.0 / bias_two)
        direction = first * (1.0 / bias_one) / (square * lax.rsqrt(square) + 1e-08)
        high = direction.astype(bf16)
        waiting = (high, (direction - high.astype(f32)).astype(bf16))
        start(f_out, first_new, i, 0)
        start(s_out, second_new, i, 1)
        if i:
            start(u_out, update, i - 1, 2)
    project(7, *waiting)
    start(u_out, update, 7, 2)
    for copy in copies:
        copy.wait()


def updated(proj, clip, projector, moment_one, moment_two):
    hbm = pl.BlockSpec(memory_space=pltpu.HBM)
    vmem = pl.BlockSpec(memory_space=pltpu.VMEM)
    return pl.pallas_call(
        update_kernel,
        name="adam_update",
        out_shape=(
            jax.ShapeDtypeStruct((32, 2048), f32),
            jax.ShapeDtypeStruct((256, 2048), f32),
            jax.ShapeDtypeStruct((256, 2048), f32),
        ),
        in_specs=[vmem] * 5,
        out_specs=(hbm, hbm, hbm),
        scratch_shapes=[
            pltpu.VMEM((32, 2048), f32),
            pltpu.VMEM((256, 2048), f32),
            pltpu.VMEM((256, 2048), f32),
            pltpu.SemaphoreType.DMA((8, 3)),
        ],
        compiler_params=pltpu.CompilerParams(vmem_limit_bytes=16 * 1024 * 1024),
        cost_estimate=pl.CostEstimate(flops=1 << 26, bytes_accessed=10 << 20, transcendentals=1 << 20),
    )(proj, clip, projector, moment_one, moment_two)


def on_device(acts, grad_out, projector, moment_one, moment_two):
    entries = float(projector.shape[1] * grad_out.shape[1] * NX)
    acts, grad_out, rows = (pltpu.with_memory_space_constraint(a, pltpu.HBM) for a in (acts, grad_out, projector))
    proj, clip = reduced(acts, grad_out, rows, entries)
    return updated(proj, clip, projector, moment_one, moment_two)


def solution(mesh):
    placed = (P("dp", None), P("dp", "group"), P("dp", None), P(None, "group"), P(None, "group"))
    return jax.shard_map(
        on_device,
        mesh=mesh,
        in_specs=placed,
        out_specs=(P("dp", "group"), P(None, "group"), P(None, "group")),
        check_vma=False,
    )
```

```python
import functools
import math

import jax
import jax.numpy as jnp
from jax import lax
from jax.experimental import pallas as pl
from jax.experimental.pallas import tpu as pltpu
from jax.sharding import PartitionSpec as P

beta_one = 0.9
beta_two = 0.95
bias_one = 1.0 - 0.9**10
bias_two = 1.0 - 0.95**10
galore_scale = 0.25

MESH = pl.DeviceIdType.MESH
NZ, NY, NX = 8, 4, 4
SPAN = 250.0
HALF = 125.0
LN2 = math.log(2.0)
NEAR = (0, 1, 7, 2, 6, 3, 5, 4)
FAR = (4, 3, 5, 2, 6, 1, 7, 0)
f32 = jnp.float32
bf16 = jnp.bfloat16


def tiles_of(block):
    return [block[16 * r : 16 * r + 16, 128 * l : 128 * l + 128] for r in range(2) for l in range(2)]


def scale_of(tiles):
    top = functools.reduce(jnp.maximum, [jnp.abs(t) for t in tiles])
    top = jnp.max(top, axis=0, keepdims=True)
    return (jnp.maximum(top, 1e-30) * 1.01).astype(bf16).astype(f32)


def encode(tiles, scale):
    rate = SPAN / scale
    out = []
    for t in tiles:
        size = jnp.exp2(jnp.abs(t) * rate - HALF)
        out.append(jnp.where(t < 0, -size, size).astype(bf16))
    return out


def decode(codes, scale):
    rate = scale * (1.0 / (SPAN * LN2))
    out = []
    for code in codes:
        code = code.astype(f32)
        size = (jnp.log(jnp.abs(code)) + HALF * LN2) * rate
        out.append(jnp.where(code < 0, -size, size))
    return out


def reduce_kernel(
    entries, acts, grad, p_hbm, proj_out, clip_out,
    p_ref, a_all, g_all, p_all, along, lhs, part,
    yb_send, yb_recv, ys_send, ys_recv, zb_send, zb_recv, column, blocks, scale_all, scale_wide, sums,
    load_sem, pair_send, pair_recv, pz_send, pz_recv, py_send, py_recv,
    yb_sent, yb_came, ys_sent, ys_came, zb_sent, zb_came, az_sent, az_came, ay_sent, ay_came,
    sy_sent, sy_came, sc_sent, sc_came, ac_sent, ac_came,
    ex_send, ex_recv, ez_send, ez_recv, ey_send, ey_recv,
):
    dp = lax.axis_index("dp")
    x = lax.axis_index("group")
    c = lax.rem(dp, 2)
    y = lax.rem(lax.div(dp, 2), NY)
    z = lax.div(dp, 2 * NY)

    def at(zz, yy, cc, xx):
        return ((zz * NY + yy) * 2 + cc, xx)

    def zoff(d):
        return lax.rem(z + d, NZ)

    def yoff(d):
        return lax.rem(y + d, NY)

    def xoff(d):
        return lax.rem(x + d, NX)

    def remote(src, dst, send, recv, device):
        return pltpu.make_async_remote_copy(
            src_ref=src, dst_ref=dst, send_sem=send, recv_sem=recv, device_id=device, device_id_type=MESH
        )

    me = at(z, y, c, x)
    sibling = at(z, y, 1 - c, x)

    def arrived(ref, recv):
        remote(ref, ref, pz_send, recv, me).wait_recv()

    def sent(ref, send):
        remote(ref, ref, send, pz_recv.at[0], me).wait_send()

    loads = [
        pltpu.make_async_copy(p_hbm, p_ref, load_sem.at[2]),
        pltpu.make_async_copy(acts, a_all.at[pl.ds(0, 512)], load_sem.at[0]),
        pltpu.make_async_copy(grad, g_all.at[pl.ds(0, 512)], load_sem.at[1]),
    ]
    for copy in loads:
        copy.start()

    barrier = pltpu.get_barrier_semaphore()
    peers = [at(zoff(d), y, cc, x) for d in NEAR[:0:-1] for cc in range(2)]
    peers += [at(z, yoff(d), cc, x) for d in range(1, NY) for cc in range(2)] + [sibling]
    peers += [at(z, y, c, xoff(d)) for d in range(1, NX)]
    for peer in peers:
        pl.semaphore_signal(barrier, inc=1, device_id=peer, device_id_type=MESH)
    loads[0].wait()
    pl.semaphore_wait(barrier, len(peers))

    mine = pl.ds(pl.multiple_of((z * NY + y) * 64 + c * 32, 32), 32)
    for cc in range(2):

        @pl.when(c != cc)
        def _():
            remote(p_ref.at[:, pl.ds(cc * 128, 128)], p_all.at[mine], pz_send, pz_recv.at[0], sibling).start()

        @pl.when(c == cc)
        def _():
            p_all[mine, :] = p_ref[:, cc * 128 : cc * 128 + 128]

    for d in NEAR[1:]:
        for cc in range(2):
            src = p_ref.at[:, pl.ds(cc * 128, 128)]
            remote(src, p_all.at[mine], pz_send, pz_recv.at[d], at(zoff(d), y, cc, x)).start()

    pair = [
        remote(acts, a_all.at[pl.ds(512, 512)], pair_send.at[0], pair_recv.at[0], sibling),
        remote(grad, g_all.at[pl.ds(512, 512)], pair_send.at[1], pair_recv.at[1], sibling),
    ]
    for copy in pair:
        copy.start()

    def p_rows(zz, yy, n=64):
        return pl.ds(pl.multiple_of((zz * NY + yy) * 64, 64), n)

    def p_forward(d):
        chunk = p_all.at[p_rows(zoff(NZ - d), y)]
        arrived(chunk if d else p_all.at[pl.ds(0, 32)], pz_recv.at[d])
        for dy in (2, 1, 3):
            remote(chunk, chunk, py_send, py_recv.at[d], at(z, yoff(dy), c, x)).start()

    def p_use(d, first):
        zz = zoff(NZ - d)
        arrived(p_all.at[pl.ds(0, 192)], py_recv.at[d])
        if first:
            loads[1].wait()
            pair[0].wait_recv()
        cols = pl.ds(pl.multiple_of(zz * 256, 256), 256)
        term = lax.dot_general(
            p_all[p_rows(zz, 0, 256), :], a_all[:, cols], (((0,), (1,)), ((), ())), preferred_element_type=f32
        )
        if first:
            along[...] = term
        else:
            along[...] += term

    lag = 4
    for k in range(NZ + lag):
        if k < NZ:
            p_forward(NEAR[k])
        if k >= lag:
            p_use(NEAR[k - lag], k == lag)

    turned = along[...]
    high = turned.astype(bf16)
    lhs[pl.ds(0, 128), :] = high
    lhs[pl.ds(128, 128), :] = (turned - high.astype(f32)).astype(bf16)
    loads[2].wait()
    pair[1].wait_recv()

    row = lax.broadcasted_iota(jnp.int32, (16, 128), 0)

    def four_tiles(k, dy):
        return tiles_of(part[k, pl.ds(pl.multiple_of(yoff(dy) * 32, 32), 32), :])

    def multiply(k):
        cols = pl.ds(pl.multiple_of(zoff(FAR[k]) * 256, 256), 256)
        both = jnp.dot(lhs[...], g_all[:, cols], preferred_element_type=f32)
        part[k] = both[:128] + both[128:]

    multiply(0)
    for k in range(NZ):
        if k < NZ - 1:
            multiply(k + 1)
        for dy in (2, 1, 3):
            tiles = four_tiles(k, dy)
            scale = scale_of(tiles)
            for i, code in enumerate(encode(tiles, scale)):
                yb_send[k, dy - 1, i] = code
            ys_send[k, dy - 1] = scale
        for dy in (2, 1, 3):
            there = at(z, yoff(dy), c, x)
            remote(yb_send.at[k, dy - 1], yb_recv.at[k, dy - 1], yb_sent, yb_came.at[k], there).start()
            remote(ys_send.at[k, dy - 1], ys_recv.at[k, dy - 1], ys_sent, ys_came.at[k], there).start()

    sent(p_all.at[pl.ds(0, 480)], pz_send)
    sent(p_all.at[pl.ds(0, 1536)], py_send)
    for copy in pair:
        copy.wait_send()

    def add(total, codes, scale):
        return [a + b for a, b in zip(total, decode(codes, scale))]

    for k, d in enumerate(FAR):
        arrived(yb_recv.at[k], yb_came.at[k])
        arrived(ys_recv.at[k], ys_came.at[k])
        total = four_tiles(k, 0)
        for i in range(NY - 1):
            total = add(total, [yb_recv[k, i, j] for j in range(4)], ys_recv[k, i])
        if d:
            message = zb_send.at[d - 1]
            scale = scale_of(total)
            for i, code in enumerate(encode(total, scale)):
                message[i] = code
            message[4] = jnp.broadcast_to(scale, (16, 128)).astype(bf16)
            remote(message, zb_recv.at[d - 1], zb_sent, zb_came.at[d], at(zoff(d), y, c, x)).start()
    sent(yb_send, yb_sent)
    sent(ys_send, ys_sent)
    for d in NEAR[1:]:
        message = zb_recv.at[d - 1]
        arrived(message, zb_came.at[d])
        total = add(total, [message[j] for j in range(4)], message[4][:1].astype(f32))

    square = functools.reduce(jnp.add, [t * t for t in total])
    sums[0] = square[:8] + square[8:]
    scale = scale_of(total)
    packet = column.at[z]
    for i, code in enumerate(encode(total, scale)):
        packet[i] = code
    packet[4] = jnp.broadcast_to(scale, (16, 128)).astype(bf16)
    for d in (2, 1, 3):
        remote(sums.at[0], sums.at[d], ex_send, ex_recv, at(z, y, c, xoff(d))).start()
    for d in NEAR[1:]:
        remote(packet, packet, az_sent, az_came.at[d], at(zoff(d), y, c, x)).start()

    def out_forward(d):
        zz = zoff(NZ - d)
        if d:
            arrived(column.at[zz], az_came.at[d])
        block = column.at[zz, pl.ds(0, 4)]
        for dy in (2, 1, 3):
            remote(block, blocks.at[c, zz, y], ay_sent, ay_came.at[d], at(z, yoff(dy), c, x)).start()
        blocks[c, zz, y] = column[zz, pl.ds(0, 4)]

    def out_share(d):
        block = blocks.at[c, zoff(NZ - d)]
        arrived(blocks.at[c, zoff(NZ - d), pl.ds(0, 3)], ay_came.at[d])
        remote(block, block, ac_sent, ac_came.at[d], sibling).start()

    for k in range(NZ):
        out_forward(NEAR[k])
        if k == 2:
            arrived(sums.at[pl.ds(0, 3)], ex_recv)
            sums[4] = sums[0] + sums[1] + sums[2] + sums[3]
            for d in NEAR[:0:-1]:
                remote(sums.at[4], sums.at[4 + d], ez_send, ez_recv, at(zoff(d), y, c, x)).start()

    tiles = [column[zz, 4] for zz in range(NZ)]
    scale_all[c, y] = functools.reduce(lambda a, b: jnp.where(row == b, tiles[b], a), range(1, NZ), tiles[0])
    for dy in (2, 1, 3):
        block = scale_all.at[c, y]
        remote(block, block, sy_sent, sy_came, at(z, yoff(dy), c, x)).start()
    arrived(sums.at[pl.ds(0, 7)], ez_recv)
    sums[12] = functools.reduce(jnp.add, [sums[i] for i in range(4, 12)])
    slot = 13
    for dy in (2, 1, 3, 0):
        for dc in (1, 0):
            if dy or dc:
                cc = lax.rem(c + dc, 2)
                remote(sums.at[12], sums.at[slot], ey_send, ey_recv, at(z, yoff(dy), cc, x)).start()
                slot += 1
    sent(zb_send, zb_sent)

    def widen(cc):
        scale_wide[cc] = scale_all[cc].astype(f32)

    def unpack(cc, zz):
        for yy in range(NY):
            codes = [blocks[cc, zz, yy, j] for j in range(4)]
            for i, t in enumerate(decode(codes, scale_wide[cc, yy, pl.ds(zz, 1), :])):
                rows = pl.ds(pl.multiple_of(cc * 128 + yy * 32 + (i // 2) * 16, 16), 16)
                cols = pl.ds(pl.multiple_of(zz * 256 + (i % 2) * 128, 128), 128)
                proj_out[rows, cols] = t

    def near(k):
        return lax.rem(jnp.where(lax.rem(k, 2) == 1, lax.div(k + 1, 2), NZ - lax.div(k, 2)), NZ)

    def unpack_own(k, carry):
        unpack(c, zoff(NZ - near(k)))
        return carry

    def unpack_theirs(k, carry):
        d = near(k)
        zz = zoff(NZ - d)
        arrived(blocks.at[1 - c, zz], ac_came.at[d])
        unpack(1 - c, zz)
        return carry

    for k in range(NZ - 2):
        out_share(NEAR[k])
    arrived(scale_all.at[c, pl.ds(0, 3)], sy_came)
    remote(scale_all.at[c], scale_all.at[c], sc_sent, sc_came, sibling).start()
    widen(c)
    lax.fori_loop(0, NZ // 2, unpack_own, 0)
    for k in range(NZ - 2, NZ):
        out_share(NEAR[k])
    lax.fori_loop(NZ // 2, NZ, unpack_own, 0)
    arrived(scale_all.at[1 - c], sc_came)
    widen(1 - c)
    lax.fori_loop(0, NZ - 2, unpack_theirs, 0)
    arrived(sums.at[pl.ds(0, 7)], ey_recv)
    energy = functools.reduce(jnp.add, [sums[i] for i in range(12, 20)])
    mean = jnp.full((8, 128), jnp.sum(energy) / entries + 1e-06, f32)
    clip_out[...] = jnp.minimum(1.0, 1.0 / jnp.sqrt(mean))
    lax.fori_loop(NZ - 2, NZ, unpack_theirs, 0)

    sent(column.at[pl.ds(0, 7)], az_sent)
    sent(blocks.at[0, pl.ds(0, 6)], ay_sent)
    sent(scale_all.at[0, pl.ds(0, 3)], sy_sent)
    sent(scale_all.at[0], sc_sent)
    sent(blocks.at[0], ac_sent)
    sent(sums.at[pl.ds(0, 3)], ex_send)
    sent(sums.at[pl.ds(0, 7)], ez_send)
    sent(sums.at[pl.ds(0, 7)], ey_send)


def reduced(acts, grad_out, projector, entries):
    sem = pltpu.SemaphoreType.DMA
    hbm = pl.BlockSpec(memory_space=pltpu.HBM)
    vmem = pl.BlockSpec(memory_space=pltpu.VMEM)
    return pl.pallas_call(
        functools.partial(reduce_kernel, entries),
        name="projected_gradient",
        out_shape=(jax.ShapeDtypeStruct((256, 2048), f32), jax.ShapeDtypeStruct((8, 128), f32)),
        in_specs=[hbm, hbm, hbm],
        out_specs=(vmem, vmem),
        scratch_shapes=[
            pltpu.VMEM((32, 256), bf16),
            pltpu.VMEM((1024, 2048), bf16),
            pltpu.VMEM((1024, 2048), bf16),
            pltpu.VMEM((2048, 128), bf16),
            pltpu.VMEM((128, 1024), f32),
            pltpu.VMEM((256, 1024), bf16),
            pltpu.VMEM((NZ, 128, 256), f32),
            pltpu.VMEM((NZ, NY - 1, 4, 16, 128), bf16),
            pltpu.VMEM((NZ, NY - 1, 4, 16, 128), bf16),
            pltpu.VMEM((NZ, NY - 1, 1, 128), f32),
            pltpu.VMEM((NZ, NY - 1, 1, 128), f32),
            pltpu.VMEM((NZ - 1, 5, 16, 128), bf16),
            pltpu.VMEM((NZ - 1, 5, 16, 128), bf16),
            pltpu.VMEM((NZ, 5, 16, 128), bf16),
            pltpu.VMEM((2, NZ, NY, 4, 16, 128), bf16),
            pltpu.VMEM((2, NY, 16, 128), bf16),
            pltpu.VMEM((2, NY, 16, 128), f32),
            pltpu.VMEM((20, 8, 128), f32),
            sem((3,)), sem((2,)), sem((2,)), sem, sem((NZ,)), sem, sem((NZ,)),
            sem, sem((NZ,)), sem, sem((NZ,)), sem, sem((NZ,)), sem, sem((NZ,)), sem, sem((NZ,)),
            sem, sem, sem, sem, sem, sem((NZ,)),
            sem, sem, sem, sem, sem, sem,
        ],
        compiler_params=pltpu.CompilerParams(
            collective_id=0, has_side_effects=True, vmem_limit_bytes=20 * 1024 * 1024
        ),
        cost_estimate=pl.CostEstimate(flops=1 << 31, bytes_accessed=6 << 20, transcendentals=1 << 20),
    )(acts, grad_out, projector)


def update_kernel(
    proj, clip, projector, first_old, second_old, update, first_new, second_new, u_out, f_out, s_out, sem
):
    scale = clip[:1, :]
    scale = jnp.concatenate([scale, scale], axis=1)
    rows = projector[...]
    copies = []

    def start(src, dst, i, j):
        cols = pl.ds(256 * i, 256)
        copies.append(pltpu.make_async_copy(src.at[:, cols], dst.at[:, cols], sem.at[i, j]))
        copies[-1].start()

    def project(i, high, low):
        moved = jnp.dot(rows, high, preferred_element_type=f32) + jnp.dot(rows, low, preferred_element_type=f32)
        u_out[:, pl.ds(256 * i, 256)] = galore_scale * moved

    waiting = None
    for i in range(8):
        cols = pl.ds(256 * i, 256)
        if i:
            project(i - 1, *waiting)
        clipped = scale * proj[:, cols]
        first = beta_one * first_old[:, cols] + (1.0 - beta_one) * clipped
        second = beta_two * second_old[:, cols] + (1.0 - beta_two) * clipped * clipped
        f_out[:, cols] = first
        s_out[:, cols] = second
        square = second * (1.0 / bias_two)
        direction = first * (1.0 / bias_one) / (square * lax.rsqrt(square) + 1e-08)
        high = direction.astype(bf16)
        waiting = (high, (direction - high.astype(f32)).astype(bf16))
        start(f_out, first_new, i, 0)
        start(s_out, second_new, i, 1)
        if i:
            start(u_out, update, i - 1, 2)
    project(7, *waiting)
    start(u_out, update, 7, 2)
    for copy in copies:
        copy.wait()


def updated(proj, clip, projector, moment_one, moment_two):
    hbm = pl.BlockSpec(memory_space=pltpu.HBM)
    vmem = pl.BlockSpec(memory_space=pltpu.VMEM)
    return pl.pallas_call(
        update_kernel,
        name="adam_update",
        out_shape=(
            jax.ShapeDtypeStruct((32, 2048), f32),
            jax.ShapeDtypeStruct((256, 2048), f32),
            jax.ShapeDtypeStruct((256, 2048), f32),
        ),
        in_specs=[vmem] * 5,
        out_specs=(hbm, hbm, hbm),
        scratch_shapes=[
            pltpu.VMEM((32, 2048), f32),
            pltpu.VMEM((256, 2048), f32),
            pltpu.VMEM((256, 2048), f32),
            pltpu.SemaphoreType.DMA((8, 3)),
        ],
        compiler_params=pltpu.CompilerParams(vmem_limit_bytes=16 * 1024 * 1024),
        cost_estimate=pl.CostEstimate(flops=1 << 26, bytes_accessed=10 << 20, transcendentals=1 << 20),
    )(proj, clip, projector, moment_one, moment_two)


def on_device(acts, grad_out, projector, moment_one, moment_two):
    entries = float(projector.shape[1] * grad_out.shape[1] * NX)
    acts, grad_out, rows = (pltpu.with_memory_space_constraint(a, pltpu.HBM) for a in (acts, grad_out, projector))
    proj, clip = reduced(acts, grad_out, rows, entries)
    return updated(proj, clip, projector, moment_one, moment_two)


def solution(mesh):
    placed = (P("dp", None), P("dp", "group"), P("dp", None), P(None, "group"), P(None, "group"))
    return jax.shard_map(
        on_device,
        mesh=mesh,
        in_specs=placed,
        out_specs=(P("dp", "group"), P(None, "group"), P(None, "group")),
        check_vma=False,
    )
```

```python
import functools
import math

import jax
import jax.numpy as jnp
from jax import lax
from jax.experimental import pallas as pl
from jax.experimental.pallas import tpu as pltpu
from jax.sharding import PartitionSpec as P

beta_one = 0.9
beta_two = 0.95
bias_one = 1.0 - 0.9**10
bias_two = 1.0 - 0.95**10
galore_scale = 0.25

MESH = pl.DeviceIdType.MESH
NZ, NY, NX = 8, 4, 4
SPAN = 250.0
HALF = 125.0
LN2 = math.log(2.0)
NEAR = (0, 1, 7, 2, 6, 3, 5, 4)
FAR = (4, 3, 5, 2, 6, 1, 7, 0)
f32 = jnp.float32
bf16 = jnp.bfloat16


def tiles_of(block):
    return [block[16 * r : 16 * r + 16, 128 * l : 128 * l + 128] for r in range(2) for l in range(2)]


def scale_of(tiles):
    top = functools.reduce(jnp.maximum, [jnp.abs(t) for t in tiles])
    top = jnp.max(top, axis=0, keepdims=True)
    return (jnp.maximum(top, 1e-30) * 1.01).astype(bf16).astype(f32)


def encode(tiles, scale):
    rate = SPAN / scale
    out = []
    for t in tiles:
        size = jnp.exp2(jnp.abs(t) * rate - HALF)
        out.append(jnp.where(t < 0, -size, size).astype(bf16))
    return out


def decode(codes, scale):
    rate = scale * (1.0 / (SPAN * LN2))
    out = []
    for code in codes:
        code = code.astype(f32)
        size = (jnp.log(jnp.abs(code)) + HALF * LN2) * rate
        out.append(jnp.where(code < 0, -size, size))
    return out


def reduce_kernel(
    entries, acts, grad, p_hbm, proj_out, clip_out,
    p_ref, a_all, g_all, p_all, along, lhs, part,
    yb_send, yb_recv, ys_send, ys_recv, zb_send, zb_recv, zs_send, zs_recv, blocks, scales, sums,
    load_sem, pair_send, pair_recv, pz_send, pz_recv, py_send, py_recv,
    yb_sent, yb_came, ys_sent, ys_came, zb_sent, zb_came, zs_sent, zs_came,
    az_sent, az_came, ay_sent, ay_came, sz_sent, sz_came, sy_sent, sy_came, sc_sent, sc_came, ac_sent, ac_came,
    ex_send, ex_recv, ez_send, ez_recv, ey_send, ey_recv,
):
    dp = lax.axis_index("dp")
    x = lax.axis_index("group")
    c = lax.rem(dp, 2)
    y = lax.rem(lax.div(dp, 2), NY)
    z = lax.div(dp, 2 * NY)

    def at(zz, yy, cc, xx):
        return ((zz * NY + yy) * 2 + cc, xx)

    way = 1 - 2 * c

    def zoff(d):
        return lax.rem(z + way * d + NZ, NZ)

    def yoff(d):
        return lax.rem(y + way * d + NY, NY)

    def xoff(d):
        return lax.rem(x + d, NX)

    def remote(src, dst, send, recv, device):
        return pltpu.make_async_remote_copy(
            src_ref=src, dst_ref=dst, send_sem=send, recv_sem=recv, device_id=device, device_id_type=MESH
        )

    me = at(z, y, c, x)
    sibling = at(z, y, 1 - c, x)

    def arrived(ref, recv):
        remote(ref, ref, pz_send, recv, me).wait_recv()

    def sent(ref, send):
        remote(ref, ref, send, pz_recv.at[0], me).wait_send()

    loads = [
        pltpu.make_async_copy(p_hbm, p_ref, load_sem.at[2]),
        pltpu.make_async_copy(acts, a_all.at[pl.ds(0, 512)], load_sem.at[0]),
        pltpu.make_async_copy(grad, g_all.at[pl.ds(0, 512)], load_sem.at[1]),
    ]
    for copy in loads:
        copy.start()

    barrier = pltpu.get_barrier_semaphore()
    peers = [at(zoff(d), y, cc, x) for d in NEAR[:0:-1] for cc in range(2)]
    peers += [at(z, yoff(d), cc, x) for d in range(1, NY) for cc in range(2)] + [sibling]
    peers += [at(z, y, c, xoff(d)) for d in range(1, NX)]
    for peer in peers:
        pl.semaphore_signal(barrier, inc=1, device_id=peer, device_id_type=MESH)
    loads[0].wait()
    pl.semaphore_wait(barrier, len(peers))

    mine = pl.ds(pl.multiple_of((z * NY + y) * 64 + c * 32, 32), 32)
    for cc in range(2):

        @pl.when(c != cc)
        def _():
            remote(p_ref.at[:, pl.ds(cc * 128, 128)], p_all.at[mine], pz_send, pz_recv.at[0], sibling).start()

        @pl.when(c == cc)
        def _():
            p_all[mine, :] = p_ref[:, cc * 128 : cc * 128 + 128]

    for d in NEAR[1:]:
        for cc in range(2):
            src = p_ref.at[:, pl.ds(cc * 128, 128)]
            seen = jnp.where(c == cc, d, NZ - d)
            remote(src, p_all.at[mine], pz_send, pz_recv.at[seen], at(zoff(d), y, cc, x)).start()

    pair = [
        remote(acts, a_all.at[pl.ds(512, 512)], pair_send.at[0], pair_recv.at[0], sibling),
        remote(grad, g_all.at[pl.ds(512, 512)], pair_send.at[1], pair_recv.at[1], sibling),
    ]
    for copy in pair:
        copy.start()

    def p_rows(zz, yy, n=64):
        return pl.ds(pl.multiple_of((zz * NY + yy) * 64, 64), n)

    def p_forward(d):
        chunk = p_all.at[p_rows(zoff(NZ - d), y)]
        arrived(chunk if d else p_all.at[pl.ds(0, 32)], pz_recv.at[d])
        for dy in (2, 1, 3):
            remote(chunk, chunk, py_send, py_recv.at[d], at(z, yoff(dy), c, x)).start()

    def p_use(d, first):
        zz = zoff(NZ - d)
        arrived(p_all.at[pl.ds(0, 192)], py_recv.at[d])
        if first:
            loads[1].wait()
            pair[0].wait_recv()
        cols = pl.ds(pl.multiple_of(zz * 256, 256), 256)
        term = lax.dot_general(
            p_all[p_rows(zz, 0, 256), :], a_all[:, cols], (((0,), (1,)), ((), ())), preferred_element_type=f32
        )
        if first:
            along[...] = term
        else:
            along[...] += term

    lag = 4
    for k in range(NZ + lag):
        if k < NZ:
            p_forward(NEAR[k])
        if k >= lag:
            p_use(NEAR[k - lag], k == lag)

    turned = along[...]
    high = turned.astype(bf16)
    lhs[pl.ds(0, 128), :] = high
    lhs[pl.ds(128, 128), :] = (turned - high.astype(f32)).astype(bf16)
    loads[2].wait()
    pair[1].wait_recv()

    def four_tiles(k, dy):
        return tiles_of(part[k, pl.ds(pl.multiple_of(yoff(dy) * 32, 32), 32), :])

    def multiply(k):
        cols = pl.ds(pl.multiple_of(zoff(FAR[k]) * 256, 256), 256)
        both = jnp.dot(lhs[...], g_all[:, cols], preferred_element_type=f32)
        part[k] = both[:128] + both[128:]

    multiply(0)
    for k in range(NZ):
        if k < NZ - 1:
            multiply(k + 1)
        for dy in (2, 1, 3):
            tiles = four_tiles(k, dy)
            scale = scale_of(tiles)
            for i, code in enumerate(encode(tiles, scale)):
                yb_send[k, dy - 1, i] = code
            ys_send[k, dy - 1] = scale
        for dy in (2, 1, 3):
            there = at(z, yoff(dy), c, x)
            remote(yb_send.at[k, dy - 1], yb_recv.at[k, dy - 1], yb_sent, yb_came.at[k], there).start()
            remote(ys_send.at[k, dy - 1], ys_recv.at[k, dy - 1], ys_sent, ys_came.at[k], there).start()

    sent(p_all.at[pl.ds(0, 480)], pz_send)
    sent(p_all.at[pl.ds(0, 1536)], py_send)
    for copy in pair:
        copy.wait_send()

    def add(total, codes, scale):
        return [a + b for a, b in zip(total, decode(codes, scale))]

    for k, d in enumerate(FAR):
        arrived(yb_recv.at[k], yb_came.at[k])
        arrived(ys_recv.at[k], ys_came.at[k])
        total = four_tiles(k, 0)
        for i in range(NY - 1):
            total = add(total, [yb_recv[k, i, j] for j in range(4)], ys_recv[k, i])
        if d:
            scale = scale_of(total)
            for i, code in enumerate(encode(total, scale)):
                zb_send[d - 1, i] = code
            zs_send[d - 1] = scale
            there = at(zoff(d), y, c, x)
            remote(zb_send.at[d - 1], zb_recv.at[d - 1], zb_sent, zb_came.at[d], there).start()
            remote(zs_send.at[d - 1], zs_recv.at[d - 1], zs_sent, zs_came.at[d], there).start()
    sent(yb_send, yb_sent)
    sent(ys_send, ys_sent)
    for d in NEAR[1:]:
        arrived(zb_recv.at[d - 1], zb_came.at[d])
        arrived(zs_recv.at[d - 1], zs_came.at[d])
        total = add(total, [zb_recv[d - 1, j] for j in range(4)], zs_recv[d - 1])

    square = functools.reduce(jnp.add, [t * t for t in total])
    sums[0] = square[:8] + square[8:]
    scale = scale_of(total)
    mine_out = blocks.at[c, z, y]
    for i, code in enumerate(encode(total, scale)):
        mine_out[i] = code
    scales[c, y, z] = scale
    for d in (2, 1, 3):
        remote(sums.at[0], sums.at[d], ex_send, ex_recv, at(z, y, c, xoff(d))).start()
    for d in NEAR[1:]:
        there = at(zoff(d), y, c, x)
        remote(mine_out, mine_out, az_sent, az_came.at[d], there).start()
        remote(scales.at[c, y, z], scales.at[c, y, z], sz_sent, sz_came, there).start()

    def out_forward(d):
        block = blocks.at[c, zoff(NZ - d), y]
        if d:
            arrived(block, az_came.at[d])
        remote(block, block, ac_sent, ac_came.at[d], sibling).start()
        for dy in (2, 1, 3):
            remote(block, block, ay_sent, ay_came.at[d], at(z, yoff(dy), c, x)).start()

    def out_share(d):
        block = blocks.at[c, zoff(NZ - d)]
        arrived(blocks.at[c, zoff(NZ - d), pl.ds(0, 3)], ay_came.at[d])
        for dy in range(1, NY):
            piece = blocks.at[c, zoff(NZ - d), yoff(dy)]
            remote(piece, piece, ac_sent, ac_came.at[d], sibling).start()

    for k in range(NZ):
        out_forward(NEAR[k])
        if k == 2:
            arrived(sums.at[pl.ds(0, 3)], ex_recv)
            sums[4] = sums[0] + sums[1] + sums[2] + sums[3]
            for d in NEAR[:0:-1]:
                remote(sums.at[4], sums.at[4 + d], ez_send, ez_recv, at(zoff(d), y, c, x)).start()

    arrived(scales.at[c, y, pl.ds(0, 7)], sz_came)
    for dy in (2, 1, 3):
        rows = scales.at[c, y]
        remote(rows, rows, sy_sent, sy_came, at(z, yoff(dy), c, x)).start()
    arrived(sums.at[pl.ds(0, 7)], ez_recv)
    sums[12] = functools.reduce(jnp.add, [sums[i] for i in range(4, 12)])
    slot = 13
    for dy in (2, 1, 3, 0):
        for dc in (1, 0):
            if dy or dc:
                cc = lax.rem(c + dc, 2)
                remote(sums.at[12], sums.at[slot], ey_send, ey_recv, at(z, yoff(dy), cc, x)).start()
                slot += 1
    sent(zb_send, zb_sent)
    sent(zs_send, zs_sent)

    def unpack(cc, zz):
        for yy in range(NY):
            codes = [blocks[cc, zz, yy, j] for j in range(4)]
            for i, t in enumerate(decode(codes, scales[cc, yy, zz])):
                rows = pl.ds(pl.multiple_of(cc * 128 + yy * 32 + (i // 2) * 16, 16), 16)
                cols = pl.ds(pl.multiple_of(zz * 256 + (i % 2) * 128, 128), 128)
                proj_out[rows, cols] = t

    def near(k):
        return lax.rem(jnp.where(lax.rem(k, 2) == 1, lax.div(k + 1, 2), NZ - lax.div(k, 2)), NZ)

    def unpack_own(k, carry):
        unpack(c, zoff(NZ - near(k)))
        return carry

    def unpack_theirs(k, carry):
        d = near(k)
        zz = zoff(d)
        arrived(blocks.at[1 - c, zz], ac_came.at[d])
        unpack(1 - c, zz)
        return carry

    for k in range(NZ):
        out_share(NEAR[k])
        if k == 4:
            arrived(scales.at[c, pl.ds(0, 3)], sy_came)
            remote(scales.at[c], scales.at[c], sc_sent, sc_came, sibling).start()
    lax.fori_loop(0, NZ, unpack_own, 0)
    arrived(scales.at[1 - c], sc_came)
    lax.fori_loop(0, NZ - 2, unpack_theirs, 0)
    arrived(sums.at[pl.ds(0, 7)], ey_recv)
    energy = functools.reduce(jnp.add, [sums[i] for i in range(12, 20)])
    mean = jnp.full((8, 128), jnp.sum(energy) / entries + 1e-06, f32)
    clip_out[...] = jnp.minimum(1.0, 1.0 / jnp.sqrt(mean))
    lax.fori_loop(NZ - 2, NZ, unpack_theirs, 0)

    sent(zb_send, az_sent)
    sent(zs_send, sz_sent)
    sent(blocks.at[0, pl.ds(0, 6)], ay_sent)
    sent(scales.at[0, pl.ds(0, 3)], sy_sent)
    sent(scales.at[0], sc_sent)
    sent(blocks.at[0], ac_sent)
    sent(sums.at[pl.ds(0, 3)], ex_send)
    sent(sums.at[pl.ds(0, 7)], ez_send)
    sent(sums.at[pl.ds(0, 7)], ey_send)


def reduced(acts, grad_out, projector, entries):
    sem = pltpu.SemaphoreType.DMA
    hbm = pl.BlockSpec(memory_space=pltpu.HBM)
    vmem = pl.BlockSpec(memory_space=pltpu.VMEM)
    return pl.pallas_call(
        functools.partial(reduce_kernel, entries),
        name="projected_gradient",
        out_shape=(jax.ShapeDtypeStruct((256, 2048), f32), jax.ShapeDtypeStruct((8, 128), f32)),
        in_specs=[hbm, hbm, hbm],
        out_specs=(vmem, vmem),
        scratch_shapes=[
            pltpu.VMEM((32, 256), bf16),
            pltpu.VMEM((1024, 2048), bf16),
            pltpu.VMEM((1024, 2048), bf16),
            pltpu.VMEM((2048, 128), bf16),
            pltpu.VMEM((128, 1024), f32),
            pltpu.VMEM((256, 1024), bf16),
            pltpu.VMEM((NZ, 128, 256), f32),
            pltpu.VMEM((NZ, NY - 1, 4, 16, 128), bf16),
            pltpu.VMEM((NZ, NY - 1, 4, 16, 128), bf16),
            pltpu.VMEM((NZ, NY - 1, 1, 128), f32),
            pltpu.VMEM((NZ, NY - 1, 1, 128), f32),
            pltpu.VMEM((NZ - 1, 4, 16, 128), bf16),
            pltpu.VMEM((NZ - 1, 4, 16, 128), bf16),
            pltpu.VMEM((NZ - 1, 1, 128), f32),
            pltpu.VMEM((NZ - 1, 1, 128), f32),
            pltpu.VMEM((2, NZ, NY, 4, 16, 128), bf16),
            pltpu.VMEM((2, NY, NZ, 1, 128), f32),
            pltpu.VMEM((20, 8, 128), f32),
            sem((3,)), sem((2,)), sem((2,)), sem, sem((NZ,)), sem, sem((NZ,)),
            sem, sem((NZ,)), sem, sem((NZ,)), sem, sem((NZ,)), sem, sem((NZ,)),
            sem, sem((NZ,)), sem, sem((NZ,)), sem, sem, sem, sem, sem, sem, sem, sem((NZ,)),
            sem, sem, sem, sem, sem, sem,
        ],
        compiler_params=pltpu.CompilerParams(
            collective_id=0, has_side_effects=True, vmem_limit_bytes=20 * 1024 * 1024
        ),
        cost_estimate=pl.CostEstimate(flops=1 << 31, bytes_accessed=6 << 20, transcendentals=1 << 20),
    )(acts, grad_out, projector)


def update_kernel(
    proj, clip, projector, first_old, second_old, update, first_new, second_new, u_out, f_out, s_out, sem
):
    scale = clip[:1, :]
    scale = jnp.concatenate([scale, scale], axis=1)
    rows = projector[...]
    copies = []

    def start(src, dst, i, j):
        cols = pl.ds(256 * i, 256)
        copies.append(pltpu.make_async_copy(src.at[:, cols], dst.at[:, cols], sem.at[i, j]))
        copies[-1].start()

    def project(i, high, low):
        moved = jnp.dot(rows, high, preferred_element_type=f32) + jnp.dot(rows, low, preferred_element_type=f32)
        u_out[:, pl.ds(256 * i, 256)] = galore_scale * moved

    waiting = None
    for i in range(8):
        cols = pl.ds(256 * i, 256)
        if i:
            project(i - 1, *waiting)
        clipped = scale * proj[:, cols]
        first = beta_one * first_old[:, cols] + (1.0 - beta_one) * clipped
        second = beta_two * second_old[:, cols] + (1.0 - beta_two) * clipped * clipped
        f_out[:, cols] = first
        s_out[:, cols] = second
        square = second * (1.0 / bias_two)
        direction = first * (1.0 / bias_one) / (square * lax.rsqrt(square) + 1e-08)
        high = direction.astype(bf16)
        waiting = (high, (direction - high.astype(f32)).astype(bf16))
        start(f_out, first_new, i, 0)
        start(s_out, second_new, i, 1)
        if i:
            start(u_out, update, i - 1, 2)
    project(7, *waiting)
    start(u_out, update, 7, 2)
    for copy in copies:
        copy.wait()


def updated(proj, clip, projector, moment_one, moment_two):
    hbm = pl.BlockSpec(memory_space=pltpu.HBM)
    vmem = pl.BlockSpec(memory_space=pltpu.VMEM)
    return pl.pallas_call(
        update_kernel,
        name="adam_update",
        out_shape=(
            jax.ShapeDtypeStruct((32, 2048), f32),
            jax.ShapeDtypeStruct((256, 2048), f32),
            jax.ShapeDtypeStruct((256, 2048), f32),
        ),
        in_specs=[vmem] * 5,
        out_specs=(hbm, hbm, hbm),
        scratch_shapes=[
            pltpu.VMEM((32, 2048), f32),
            pltpu.VMEM((256, 2048), f32),
            pltpu.VMEM((256, 2048), f32),
            pltpu.SemaphoreType.DMA((8, 3)),
        ],
        compiler_params=pltpu.CompilerParams(vmem_limit_bytes=16 * 1024 * 1024),
        cost_estimate=pl.CostEstimate(flops=1 << 26, bytes_accessed=10 << 20, transcendentals=1 << 20),
    )(proj, clip, projector, moment_one, moment_two)


def on_device(acts, grad_out, projector, moment_one, moment_two):
    entries = float(projector.shape[1] * grad_out.shape[1] * NX)
    acts, grad_out, rows = (pltpu.with_memory_space_constraint(a, pltpu.HBM) for a in (acts, grad_out, projector))
    proj, clip = reduced(acts, grad_out, rows, entries)
    return updated(proj, clip, projector, moment_one, moment_two)


def solution(mesh):
    placed = (P("dp", None), P("dp", "group"), P("dp", None), P(None, "group"), P(None, "group"))
    return jax.shard_map(
        on_device,
        mesh=mesh,
        in_specs=placed,
        out_specs=(P("dp", "group"), P(None, "group"), P(None, "group")),
        check_vma=False,
    )
```

```python
import functools
import math

import jax
import jax.numpy as jnp
from jax import lax
from jax.experimental import pallas as pl
from jax.experimental.pallas import tpu as pltpu
from jax.sharding import PartitionSpec as P

beta_one = 0.9
beta_two = 0.95
bias_one = 1.0 - 0.9**10
bias_two = 1.0 - 0.95**10
galore_scale = 0.25

MESH = pl.DeviceIdType.MESH
NZ, NY, NX = 8, 4, 4
SPAN = 250.0
HALF = 125.0
LN2 = math.log(2.0)
NEAR = (0, 1, 7, 2, 6, 3, 5, 4)
FAR = (4, 3, 5, 2, 6, 1, 7, 0)
f32 = jnp.float32
bf16 = jnp.bfloat16


def tiles_of(block):
    return [block[16 * r : 16 * r + 16, 128 * l : 128 * l + 128] for r in range(2) for l in range(2)]


def scale_of(tiles):
    top = functools.reduce(jnp.maximum, [jnp.abs(t) for t in tiles])
    top = jnp.max(top, axis=0, keepdims=True)
    return (jnp.maximum(top, 1e-30) * 1.01).astype(bf16).astype(f32)


def encode(tiles, scale):
    rate = SPAN / scale
    out = []
    for t in tiles:
        size = jnp.exp2(jnp.abs(t) * rate - HALF)
        out.append(jnp.where(t < 0, -size, size).astype(bf16))
    return out


def decode(codes, scale):
    rate = scale * (1.0 / (SPAN * LN2))
    out = []
    for code in codes:
        code = code.astype(f32)
        size = (jnp.log(jnp.abs(code)) + HALF * LN2) * rate
        out.append(jnp.where(code < 0, -size, size))
    return out


def reduce_kernel(
    entries, acts, grad, p_hbm, proj_out, clip_out,
    p_ref, a_all, g_all, p_all, along, lhs, part,
    yb_send, yb_recv, ys_send, ys_recv, zb_send, zb_recv, zs_send, zs_recv, blocks, scales, sums,
    load_sem, pair_send, pair_recv, pz_send, pz_recv, py_send, py_recv,
    yb_sent, yb_came, ys_sent, ys_came, zb_sent, zb_came, zs_sent, zs_came,
    az_sent, az_came, ay_sent, ay_came, sz_sent, sz_came, sy_sent, sy_came, sc_sent, sc_came, ac_sent, ac_came,
    ex_send, ex_recv, ez_send, ez_recv, ey_send, ey_recv,
):
    dp = lax.axis_index("dp")
    x = lax.axis_index("group")
    c = lax.rem(dp, 2)
    y = lax.rem(lax.div(dp, 2), NY)
    z = lax.div(dp, 2 * NY)

    def at(zz, yy, cc, xx):
        return ((zz * NY + yy) * 2 + cc, xx)

    way = 1 - 2 * c

    def zoff(d):
        return lax.rem(z + way * d + NZ, NZ)

    def yoff(d):
        return lax.rem(y + way * d + NY, NY)

    def xoff(d):
        return lax.rem(x + d, NX)

    def remote(src, dst, send, recv, device):
        return pltpu.make_async_remote_copy(
            src_ref=src, dst_ref=dst, send_sem=send, recv_sem=recv, device_id=device, device_id_type=MESH
        )

    me = at(z, y, c, x)
    sibling = at(z, y, 1 - c, x)

    def arrived(ref, recv):
        remote(ref, ref, pz_send, recv, me).wait_recv()

    def sent(ref, send):
        remote(ref, ref, send, pz_recv.at[0], me).wait_send()

    loads = [
        pltpu.make_async_copy(p_hbm, p_ref, load_sem.at[2]),
        pltpu.make_async_copy(acts, a_all.at[pl.ds(0, 512)], load_sem.at[0]),
        pltpu.make_async_copy(grad, g_all.at[pl.ds(0, 512)], load_sem.at[1]),
    ]
    for copy in loads:
        copy.start()

    barrier = pltpu.get_barrier_semaphore()
    peers = [at(zoff(d), y, cc, x) for d in NEAR[:0:-1] for cc in range(2)]
    peers += [at(z, yoff(d), cc, x) for d in range(1, NY) for cc in range(2)] + [sibling]
    peers += [at(z, y, c, xoff(d)) for d in range(1, NX)]
    for peer in peers:
        pl.semaphore_signal(barrier, inc=1, device_id=peer, device_id_type=MESH)
    loads[0].wait()
    pl.semaphore_wait(barrier, len(peers))

    mine = pl.ds(pl.multiple_of((z * NY + y) * 64 + c * 32, 32), 32)
    for cc in range(2):

        @pl.when(c != cc)
        def _():
            remote(p_ref.at[:, pl.ds(cc * 128, 128)], p_all.at[mine], pz_send, pz_recv.at[0], sibling).start()

        @pl.when(c == cc)
        def _():
            p_all[mine, :] = p_ref[:, cc * 128 : cc * 128 + 128]

    for d in NEAR[1:]:
        for cc in range(2):
            src = p_ref.at[:, pl.ds(cc * 128, 128)]
            seen = jnp.where(c == cc, d, NZ - d)
            remote(src, p_all.at[mine], pz_send, pz_recv.at[seen], at(zoff(d), y, cc, x)).start()

    pair = [
        remote(acts, a_all.at[pl.ds(512, 512)], pair_send.at[0], pair_recv.at[0], sibling),
        remote(grad, g_all.at[pl.ds(512, 512)], pair_send.at[1], pair_recv.at[1], sibling),
    ]
    for copy in pair:
        copy.start()

    def p_rows(zz, yy, n=64):
        return pl.ds(pl.multiple_of((zz * NY + yy) * 64, 64), n)

    def p_forward(d):
        chunk = p_all.at[p_rows(zoff(NZ - d), y)]
        arrived(chunk if d else p_all.at[pl.ds(0, 32)], pz_recv.at[d])
        for dy in (2, 1, 3):
            remote(chunk, chunk, py_send, py_recv.at[d], at(z, yoff(dy), c, x)).start()

    def p_use(d, first):
        zz = zoff(NZ - d)
        arrived(p_all.at[pl.ds(0, 192)], py_recv.at[d])
        if first:
            loads[1].wait()
            pair[0].wait_recv()
        cols = pl.ds(pl.multiple_of(zz * 256, 256), 256)
        term = lax.dot_general(
            p_all[p_rows(zz, 0, 256), :], a_all[:, cols], (((0,), (1,)), ((), ())), preferred_element_type=f32
        )
        if first:
            along[...] = term
        else:
            along[...] += term

    for d in NEAR:
        p_forward(d)
    for d in NEAR:
        p_use(d, d == 0)

    turned = along[...]
    high = turned.astype(bf16)
    lhs[pl.ds(0, 128), :] = high
    lhs[pl.ds(128, 128), :] = (turned - high.astype(f32)).astype(bf16)
    loads[2].wait()
    pair[1].wait_recv()

    def four_tiles(k, dy):
        return tiles_of(part[k, pl.ds(pl.multiple_of(yoff(dy) * 32, 32), 32), :])

    def multiply(k):
        cols = pl.ds(pl.multiple_of(zoff(FAR[k]) * 256, 256), 256)
        both = jnp.dot(lhs[...], g_all[:, cols], preferred_element_type=f32)
        part[k] = both[:128] + both[128:]

    multiply(0)
    for k in range(NZ):
        if 0 < k < NZ - 1:
            multiply(k + 1)
        for dy in (2, 1, 3):
            tiles = four_tiles(k, dy)
            scale = scale_of(tiles)
            for i, code in enumerate(encode(tiles, scale)):
                yb_send[k, dy - 1, i] = code
            ys_send[k, dy - 1] = scale
        for dy in (2, 1, 3):
            there = at(z, yoff(dy), c, x)
            remote(yb_send.at[k, dy - 1], yb_recv.at[k, dy - 1], yb_sent, yb_came.at[k], there).start()
            remote(ys_send.at[k, dy - 1], ys_recv.at[k, dy - 1], ys_sent, ys_came.at[k], there).start()
        if k == 0:
            multiply(1)

    sent(p_all.at[pl.ds(0, 480)], pz_send)
    sent(p_all.at[pl.ds(0, 1536)], py_send)
    for copy in pair:
        copy.wait_send()

    def add(total, codes, scale):
        return [a + b for a, b in zip(total, decode(codes, scale))]

    for k, d in enumerate(FAR):
        arrived(yb_recv.at[k], yb_came.at[k])
        arrived(ys_recv.at[k], ys_came.at[k])
        total = four_tiles(k, 0)
        for i in range(NY - 1):
            total = add(total, [yb_recv[k, i, j] for j in range(4)], ys_recv[k, i])
        if d:
            scale = scale_of(total)
            for i, code in enumerate(encode(total, scale)):
                zb_send[d - 1, i] = code
            zs_send[d - 1] = scale
            there = at(zoff(d), y, c, x)
            remote(zb_send.at[d - 1], zb_recv.at[d - 1], zb_sent, zb_came.at[d], there).start()
            remote(zs_send.at[d - 1], zs_recv.at[d - 1], zs_sent, zs_came.at[d], there).start()
    sent(yb_send, yb_sent)
    sent(ys_send, ys_sent)
    for d in NEAR[1:]:
        arrived(zb_recv.at[d - 1], zb_came.at[d])
        arrived(zs_recv.at[d - 1], zs_came.at[d])
        total = add(total, [zb_recv[d - 1, j] for j in range(4)], zs_recv[d - 1])

    square = functools.reduce(jnp.add, [t * t for t in total])
    sums[0] = square[:8] + square[8:]
    scale = scale_of(total)
    mine_out = blocks.at[c, z, y]
    for i, code in enumerate(encode(total, scale)):
        mine_out[i] = code
    scales[c, y, z] = scale
    for d in (2, 1, 3):
        remote(sums.at[0], sums.at[d], ex_send, ex_recv, at(z, y, c, xoff(d))).start()
    for d in NEAR[1:]:
        there = at(zoff(d), y, c, x)
        remote(mine_out, mine_out, az_sent, az_came.at[d], there).start()
        remote(scales.at[c, y, z], scales.at[c, y, z], sz_sent, sz_came, there).start()

    def out_forward(d):
        block = blocks.at[c, zoff(NZ - d), y]
        if d:
            arrived(block, az_came.at[d])
        remote(block, block, ac_sent, ac_came.at[d], sibling).start()
        for dy in (2, 1, 3):
            remote(block, block, ay_sent, ay_came.at[d], at(z, yoff(dy), c, x)).start()

    def out_share(d):
        block = blocks.at[c, zoff(NZ - d)]
        arrived(blocks.at[c, zoff(NZ - d), pl.ds(0, 3)], ay_came.at[d])
        for dy in range(1, NY):
            piece = blocks.at[c, zoff(NZ - d), yoff(dy)]
            remote(piece, piece, ac_sent, ac_came.at[d], sibling).start()

    for k in range(NZ):
        out_forward(NEAR[k])
        if k == 2:
            arrived(sums.at[pl.ds(0, 3)], ex_recv)
            sums[4] = sums[0] + sums[1] + sums[2] + sums[3]
            for d in NEAR[:0:-1]:
                remote(sums.at[4], sums.at[4 + d], ez_send, ez_recv, at(zoff(d), y, c, x)).start()

    arrived(scales.at[c, y, pl.ds(0, 7)], sz_came)
    for dy in (2, 1, 3):
        rows = scales.at[c, y]
        remote(rows, rows, sy_sent, sy_came, at(z, yoff(dy), c, x)).start()
    arrived(sums.at[pl.ds(0, 7)], ez_recv)
    sums[12] = functools.reduce(jnp.add, [sums[i] for i in range(4, 12)])
    slot = 13
    for dy in (2, 1, 3, 0):
        for dc in (1, 0):
            if dy or dc:
                cc = lax.rem(c + dc, 2)
                remote(sums.at[12], sums.at[slot], ey_send, ey_recv, at(z, yoff(dy), cc, x)).start()
                slot += 1
    sent(zb_send, zb_sent)
    sent(zs_send, zs_sent)

    def unpack(cc, zz):
        for yy in range(NY):
            codes = [blocks[cc, zz, yy, j] for j in range(4)]
            for i, t in enumerate(decode(codes, scales[cc, yy, zz])):
                rows = pl.ds(pl.multiple_of(cc * 128 + yy * 32 + (i // 2) * 16, 16), 16)
                cols = pl.ds(pl.multiple_of(zz * 256 + (i % 2) * 128, 128), 128)
                proj_out[rows, cols] = t

    def near(k):
        return lax.rem(jnp.where(lax.rem(k, 2) == 1, lax.div(k + 1, 2), NZ - lax.div(k, 2)), NZ)

    def unpack_own(k, carry):
        unpack(c, zoff(NZ - near(k)))
        return carry

    def unpack_theirs(k, carry):
        d = near(k)
        zz = zoff(d)
        arrived(blocks.at[1 - c, zz], ac_came.at[d])
        unpack(1 - c, zz)
        return carry

    for k in range(NZ):
        out_share(NEAR[k])
        if k == 4:
            arrived(scales.at[c, pl.ds(0, 3)], sy_came)
            remote(scales.at[c], scales.at[c], sc_sent, sc_came, sibling).start()
    lax.fori_loop(0, NZ, unpack_own, 0)
    arrived(scales.at[1 - c], sc_came)
    lax.fori_loop(0, NZ - 2, unpack_theirs, 0)
    arrived(sums.at[pl.ds(0, 7)], ey_recv)
    energy = functools.reduce(jnp.add, [sums[i] for i in range(12, 20)])
    mean = jnp.full((8, 128), jnp.sum(energy) / entries + 1e-06, f32)
    clip_out[...] = jnp.minimum(1.0, 1.0 / jnp.sqrt(mean))
    lax.fori_loop(NZ - 2, NZ, unpack_theirs, 0)

    sent(zb_send, az_sent)
    sent(zs_send, sz_sent)
    sent(blocks.at[0, pl.ds(0, 6)], ay_sent)
    sent(scales.at[0, pl.ds(0, 3)], sy_sent)
    sent(scales.at[0], sc_sent)
    sent(blocks.at[0], ac_sent)
    sent(sums.at[pl.ds(0, 3)], ex_send)
    sent(sums.at[pl.ds(0, 7)], ez_send)
    sent(sums.at[pl.ds(0, 7)], ey_send)


def reduced(acts, grad_out, projector, entries):
    sem = pltpu.SemaphoreType.DMA
    hbm = pl.BlockSpec(memory_space=pltpu.HBM)
    vmem = pl.BlockSpec(memory_space=pltpu.VMEM)
    return pl.pallas_call(
        functools.partial(reduce_kernel, entries),
        name="projected_gradient",
        out_shape=(jax.ShapeDtypeStruct((256, 2048), f32), jax.ShapeDtypeStruct((8, 128), f32)),
        in_specs=[hbm, hbm, hbm],
        out_specs=(vmem, vmem),
        scratch_shapes=[
            pltpu.VMEM((32, 256), bf16),
            pltpu.VMEM((1024, 2048), bf16),
            pltpu.VMEM((1024, 2048), bf16),
            pltpu.VMEM((2048, 128), bf16),
            pltpu.VMEM((128, 1024), f32),
            pltpu.VMEM((256, 1024), bf16),
            pltpu.VMEM((NZ, 128, 256), f32),
            pltpu.VMEM((NZ, NY - 1, 4, 16, 128), bf16),
            pltpu.VMEM((NZ, NY - 1, 4, 16, 128), bf16),
            pltpu.VMEM((NZ, NY - 1, 1, 128), f32),
            pltpu.VMEM((NZ, NY - 1, 1, 128), f32),
            pltpu.VMEM((NZ - 1, 4, 16, 128), bf16),
            pltpu.VMEM((NZ - 1, 4, 16, 128), bf16),
            pltpu.VMEM((NZ - 1, 1, 128), f32),
            pltpu.VMEM((NZ - 1, 1, 128), f32),
            pltpu.VMEM((2, NZ, NY, 4, 16, 128), bf16),
            pltpu.VMEM((2, NY, NZ, 1, 128), f32),
            pltpu.VMEM((20, 8, 128), f32),
            sem((3,)), sem((2,)), sem((2,)), sem, sem((NZ,)), sem, sem((NZ,)),
            sem, sem((NZ,)), sem, sem((NZ,)), sem, sem((NZ,)), sem, sem((NZ,)),
            sem, sem((NZ,)), sem, sem((NZ,)), sem, sem, sem, sem, sem, sem, sem, sem((NZ,)),
            sem, sem, sem, sem, sem, sem,
        ],
        compiler_params=pltpu.CompilerParams(
            collective_id=0, has_side_effects=True, vmem_limit_bytes=20 * 1024 * 1024
        ),
        cost_estimate=pl.CostEstimate(flops=1 << 31, bytes_accessed=6 << 20, transcendentals=1 << 20),
    )(acts, grad_out, projector)


def update_kernel(
    proj, clip, projector, first_old, second_old, update, first_new, second_new, u_out, f_out, s_out, sem
):
    scale = clip[:1, :]
    scale = jnp.concatenate([scale, scale], axis=1)
    rows = jnp.concatenate([projector[...], projector[...]], axis=1)
    copies = []

    def start(src, dst, i, j):
        cols = pl.ds(256 * i, 256)
        copies.append(pltpu.make_async_copy(src.at[:, cols], dst.at[:, cols], sem.at[i, j]))
        copies[-1].start()

    def project(i, high, low):
        moved = jnp.dot(rows, jnp.concatenate([high, low], axis=0), preferred_element_type=f32)
        u_out[:, pl.ds(256 * i, 256)] = galore_scale * moved

    waiting = None
    for i in range(8):
        cols = pl.ds(256 * i, 256)
        if i:
            project(i - 1, *waiting)
        clipped = scale * proj[:, cols]
        first = beta_one * first_old[:, cols] + (1.0 - beta_one) * clipped
        second = beta_two * second_old[:, cols] + (1.0 - beta_two) * clipped * clipped
        f_out[:, cols] = first
        s_out[:, cols] = second
        square = second * (1.0 / bias_two)
        direction = first * (1.0 / bias_one) / (square * lax.rsqrt(square) + 1e-08)
        high = direction.astype(bf16)
        waiting = (high, (direction - high.astype(f32)).astype(bf16))
        start(f_out, first_new, i, 0)
        start(s_out, second_new, i, 1)
        if i:
            start(u_out, update, i - 1, 2)
    project(7, *waiting)
    start(u_out, update, 7, 2)
    for copy in copies:
        copy.wait()


def updated(proj, clip, projector, moment_one, moment_two):
    hbm = pl.BlockSpec(memory_space=pltpu.HBM)
    vmem = pl.BlockSpec(memory_space=pltpu.VMEM)
    return pl.pallas_call(
        update_kernel,
        name="adam_update",
        out_shape=(
            jax.ShapeDtypeStruct((32, 2048), f32),
            jax.ShapeDtypeStruct((256, 2048), f32),
            jax.ShapeDtypeStruct((256, 2048), f32),
        ),
        in_specs=[vmem] * 5,
        out_specs=(hbm, hbm, hbm),
        scratch_shapes=[
            pltpu.VMEM((32, 2048), f32),
            pltpu.VMEM((256, 2048), f32),
            pltpu.VMEM((256, 2048), f32),
            pltpu.SemaphoreType.DMA((8, 3)),
        ],
        compiler_params=pltpu.CompilerParams(vmem_limit_bytes=16 * 1024 * 1024),
        cost_estimate=pl.CostEstimate(flops=1 << 26, bytes_accessed=10 << 20, transcendentals=1 << 20),
    )(proj, clip, projector, moment_one, moment_two)


def on_device(acts, grad_out, projector, moment_one, moment_two):
    entries = float(projector.shape[1] * grad_out.shape[1] * NX)
    acts, grad_out, rows = (pltpu.with_memory_space_constraint(a, pltpu.HBM) for a in (acts, grad_out, projector))
    proj, clip = reduced(acts, grad_out, rows, entries)
    return updated(proj, clip, projector, moment_one, moment_two)


def solution(mesh):
    placed = (P("dp", None), P("dp", "group"), P("dp", None), P(None, "group"), P(None, "group"))
    return jax.shard_map(
        on_device,
        mesh=mesh,
        in_specs=placed,
        out_specs=(P("dp", "group"), P(None, "group"), P(None, "group")),
        check_vma=False,
    )
```

```python
import functools
import math

import jax
import jax.numpy as jnp
from jax import lax
from jax.experimental import pallas as pl
from jax.experimental.pallas import tpu as pltpu
from jax.sharding import PartitionSpec as P

beta_one = 0.9
beta_two = 0.95
bias_one = 1.0 - 0.9**10
bias_two = 1.0 - 0.95**10
galore_scale = 0.25

MESH = pl.DeviceIdType.MESH
NZ, NY, NX = 8, 4, 4
SPAN = 250.0
HALF = 125.0
LN2 = math.log(2.0)
NEAR = (0, 1, 7, 2, 6, 3, 5, 4)
FAR = (4, 3, 5, 2, 6, 1, 7, 0)
f32 = jnp.float32
bf16 = jnp.bfloat16


def tiles_of(block):
    return [block[16 * r : 16 * r + 16, 128 * l : 128 * l + 128] for r in range(2) for l in range(2)]


def scale_of(tiles):
    top = functools.reduce(jnp.maximum, [jnp.abs(t) for t in tiles])
    top = jnp.max(top, axis=0, keepdims=True)
    return (jnp.maximum(top, 1e-30) * 1.01).astype(bf16).astype(f32)


def encode(tiles, scale):
    rate = SPAN / scale
    out = []
    for t in tiles:
        size = jnp.exp2(jnp.abs(t) * rate - HALF)
        out.append(jnp.where(t < 0, -size, size).astype(bf16))
    return out


def decode(codes, scale):
    rate = scale * (1.0 / (SPAN * LN2))
    out = []
    for code in codes:
        code = code.astype(f32)
        size = (jnp.log(jnp.abs(code)) + HALF * LN2) * rate
        out.append(jnp.where(code < 0, -size, size))
    return out


def reduce_kernel(
    entries, acts, grad, p_hbm, proj_out, clip_out,
    p_ref, a_all, g_all, p_all, along, lhs, part,
    yb_send, yb_recv, ys_send, ys_recv, zb_send, zb_recv, zs_send, zs_recv, blocks, scales, sums,
    load_sem, pair_send, pair_recv, pz_send, pz_recv, py_send, py_recv,
    yb_sent, yb_came, ys_sent, ys_came, zb_sent, zb_came, zs_sent, zs_came,
    az_sent, az_came, ay_sent, ay_came, sz_sent, sz_came, sy_sent, sy_came, sc_sent, sc_came, ac_sent, ac_came,
    ex_send, ex_recv, ez_send, ez_recv, ey_send, ey_recv,
):
    dp = lax.axis_index("dp")
    x = lax.axis_index("group")
    c = lax.rem(dp, 2)
    y = lax.rem(lax.div(dp, 2), NY)
    z = lax.div(dp, 2 * NY)

    def at(zz, yy, cc, xx):
        return ((zz * NY + yy) * 2 + cc, xx)

    way = 1 - 2 * c

    def zoff(d):
        return lax.rem(z + way * d + NZ, NZ)

    def yoff(d):
        return lax.rem(y + way * d + NY, NY)

    def xoff(d):
        return lax.rem(x + d, NX)

    def remote(src, dst, send, recv, device):
        return pltpu.make_async_remote_copy(
            src_ref=src, dst_ref=dst, send_sem=send, recv_sem=recv, device_id=device, device_id_type=MESH
        )

    me = at(z, y, c, x)
    sibling = at(z, y, 1 - c, x)

    def arrived(ref, recv):
        remote(ref, ref, pz_send, recv, me).wait_recv()

    def sent(ref, send):
        remote(ref, ref, send, pz_recv.at[0], me).wait_send()

    loads = [
        pltpu.make_async_copy(p_hbm, p_ref, load_sem.at[2]),
        pltpu.make_async_copy(acts, a_all.at[pl.ds(0, 512)], load_sem.at[0]),
        pltpu.make_async_copy(grad, g_all.at[pl.ds(0, 512)], load_sem.at[1]),
    ]
    for copy in loads:
        copy.start()

    barrier = pltpu.get_barrier_semaphore()
    peers = [at(zoff(d), y, cc, x) for d in NEAR[:0:-1] for cc in range(2)]
    peers += [at(z, yoff(d), cc, x) for d in range(1, NY) for cc in range(2)] + [sibling]
    peers += [at(z, y, c, xoff(d)) for d in range(1, NX)]
    for peer in peers:
        pl.semaphore_signal(barrier, inc=1, device_id=peer, device_id_type=MESH)
    loads[0].wait()
    pl.semaphore_wait(barrier, len(peers))

    mine = pl.ds(pl.multiple_of((z * NY + y) * 64 + c * 32, 32), 32)
    for cc in range(2):

        @pl.when(c != cc)
        def _():
            remote(p_ref.at[:, pl.ds(cc * 128, 128)], p_all.at[mine], pz_send, pz_recv.at[0], sibling).start()

        @pl.when(c == cc)
        def _():
            p_all[mine, :] = p_ref[:, cc * 128 : cc * 128 + 128]

    for d in NEAR[1:]:
        for cc in range(2):
            src = p_ref.at[:, pl.ds(cc * 128, 128)]
            seen = jnp.where(c == cc, d, NZ - d)
            remote(src, p_all.at[mine], pz_send, pz_recv.at[seen], at(zoff(d), y, cc, x)).start()

    pair = [
        remote(acts, a_all.at[pl.ds(512, 512)], pair_send.at[0], pair_recv.at[0], sibling),
        remote(grad, g_all.at[pl.ds(512, 512)], pair_send.at[1], pair_recv.at[1], sibling),
    ]
    for copy in pair:
        copy.start()

    def p_rows(zz, yy, n=64):
        return pl.ds(pl.multiple_of((zz * NY + yy) * 64, 64), n)

    def p_forward(d):
        chunk = p_all.at[p_rows(zoff(NZ - d), y)]
        arrived(chunk if d else p_all.at[pl.ds(0, 32)], pz_recv.at[d])
        for dy in (2, 1, 3):
            remote(chunk, chunk, py_send, py_recv.at[d], at(z, yoff(dy), c, x)).start()

    def p_use(d, first):
        zz = zoff(NZ - d)
        arrived(p_all.at[pl.ds(0, 192)], py_recv.at[d])
        if first:
            loads[1].wait()
            pair[0].wait_recv()
        cols = pl.ds(pl.multiple_of(zz * 256, 256), 256)
        term = lax.dot_general(
            p_all[p_rows(zz, 0, 256), :], a_all[:, cols], (((0,), (1,)), ((), ())), preferred_element_type=f32
        )
        if first:
            along[...] = term
        else:
            along[...] += term

    for d in NEAR:
        p_forward(d)
    for d in NEAR:
        p_use(d, d == 0)

    turned = along[...]
    high = turned.astype(bf16)
    lhs[pl.ds(0, 128), :] = high
    lhs[pl.ds(128, 128), :] = (turned - high.astype(f32)).astype(bf16)
    loads[2].wait()
    pair[1].wait_recv()

    def four_tiles(k, dy):
        return tiles_of(part[k, pl.ds(pl.multiple_of(yoff(dy) * 32, 32), 32), :])

    def multiply(k):
        cols = pl.ds(pl.multiple_of(zoff(FAR[k]) * 256, 256), 256)
        both = jnp.dot(lhs[...], g_all[:, cols], preferred_element_type=f32)
        part[k] = both[:128] + both[128:]

    multiply(0)
    for k in range(NZ):
        if 0 < k < NZ - 1:
            multiply(k + 1)
        for dy in (2, 1, 3):
            tiles = four_tiles(k, dy)
            scale = scale_of(tiles)
            for i, code in enumerate(encode(tiles, scale)):
                yb_send[k, dy - 1, i] = code
            ys_send[k, dy - 1] = scale
        for dy in (2, 1, 3):
            there = at(z, yoff(dy), c, x)
            remote(yb_send.at[k, dy - 1], yb_recv.at[k, dy - 1], yb_sent, yb_came.at[k], there).start()
            remote(ys_send.at[k, dy - 1], ys_recv.at[k, dy - 1], ys_sent, ys_came.at[k], there).start()
        if k == 0:
            multiply(1)

    sent(p_all.at[pl.ds(0, 480)], pz_send)
    sent(p_all.at[pl.ds(0, 1536)], py_send)
    for copy in pair:
        copy.wait_send()

    def add(total, codes, scale):
        return [a + b for a, b in zip(total, decode(codes, scale))]

    for k, d in enumerate(FAR):
        arrived(yb_recv.at[k], yb_came.at[k])
        arrived(ys_recv.at[k], ys_came.at[k])
        total = four_tiles(k, 0)
        for i in range(NY - 1):
            total = add(total, [yb_recv[k, i, j] for j in range(4)], ys_recv[k, i])
        if d:
            scale = scale_of(total)
            for i, code in enumerate(encode(total, scale)):
                zb_send[d - 1, i] = code
            zs_send[d - 1] = scale
            there = at(zoff(d), y, c, x)
            remote(zb_send.at[d - 1], zb_recv.at[d - 1], zb_sent, zb_came.at[d], there).start()
            remote(zs_send.at[d - 1], zs_recv.at[d - 1], zs_sent, zs_came.at[d], there).start()
    sent(yb_send, yb_sent)
    sent(ys_send, ys_sent)
    for d in NEAR[1:]:
        arrived(zb_recv.at[d - 1], zb_came.at[d])
        arrived(zs_recv.at[d - 1], zs_came.at[d])
        total = add(total, [zb_recv[d - 1, j] for j in range(4)], zs_recv[d - 1])

    scale = scale_of(total)
    mine_out = blocks.at[c, z, y]
    for i, code in enumerate(encode(total, scale)):
        mine_out[i] = code
    scales[c, y, z] = scale
    for d in NEAR[1:]:
        there = at(zoff(d), y, c, x)
        remote(mine_out, mine_out, az_sent, az_came.at[d], there).start()
        remote(scales.at[c, y, z], scales.at[c, y, z], sz_sent, sz_came, there).start()

    square = functools.reduce(jnp.add, [t * t for t in total])
    sums[0] = square[:8] + square[8:]
    for d in (2, 1, 3):
        remote(sums.at[0], sums.at[d], ex_send, ex_recv, at(z, y, c, xoff(d))).start()

    def out_forward(d):
        block = blocks.at[c, zoff(NZ - d), y]
        if d:
            arrived(block, az_came.at[d])
        remote(block, block, ac_sent, ac_came.at[d], sibling).start()
        for dy in (2, 1, 3):
            remote(block, block, ay_sent, ay_came.at[d], at(z, yoff(dy), c, x)).start()

    def out_share(d):
        block = blocks.at[c, zoff(NZ - d)]
        arrived(blocks.at[c, zoff(NZ - d), pl.ds(0, 3)], ay_came.at[d])
        for dy in range(1, NY):
            piece = blocks.at[c, zoff(NZ - d), yoff(dy)]
            remote(piece, piece, ac_sent, ac_came.at[d], sibling).start()

    for k in range(NZ):
        out_forward(NEAR[k])
        if k == 2:
            arrived(sums.at[pl.ds(0, 3)], ex_recv)
            sums[4] = sums[0] + sums[1] + sums[2] + sums[3]
            for d in NEAR[:0:-1]:
                remote(sums.at[4], sums.at[4 + d], ez_send, ez_recv, at(zoff(d), y, c, x)).start()

    arrived(scales.at[c, y, pl.ds(0, 7)], sz_came)
    for dy in (2, 1, 3):
        rows = scales.at[c, y]
        remote(rows, rows, sy_sent, sy_came, at(z, yoff(dy), c, x)).start()
    arrived(sums.at[pl.ds(0, 7)], ez_recv)
    sums[12] = functools.reduce(jnp.add, [sums[i] for i in range(4, 12)])
    slot = 13
    for dy in (2, 1, 3, 0):
        for dc in (1, 0):
            if dy or dc:
                cc = lax.rem(c + dc, 2)
                remote(sums.at[12], sums.at[slot], ey_send, ey_recv, at(z, yoff(dy), cc, x)).start()
                slot += 1
    sent(zb_send, zb_sent)
    sent(zs_send, zs_sent)

    def unpack(cc, zz):
        for yy in range(NY):
            codes = [blocks[cc, zz, yy, j] for j in range(4)]
            for i, t in enumerate(decode(codes, scales[cc, yy, zz])):
                rows = pl.ds(pl.multiple_of(cc * 128 + yy * 32 + (i // 2) * 16, 16), 16)
                cols = pl.ds(pl.multiple_of(zz * 256 + (i % 2) * 128, 128), 128)
                proj_out[rows, cols] = t

    def near(k):
        return lax.rem(jnp.where(lax.rem(k, 2) == 1, lax.div(k + 1, 2), NZ - lax.div(k, 2)), NZ)

    def unpack_own(k, carry):
        unpack(c, zoff(NZ - near(k)))
        return carry

    def unpack_theirs(k, carry):
        d = near(k)
        zz = zoff(d)
        arrived(blocks.at[1 - c, zz], ac_came.at[d])
        unpack(1 - c, zz)
        return carry

    for k in range(NZ):
        out_share(NEAR[k])
        if k == 4:
            arrived(scales.at[c, pl.ds(0, 3)], sy_came)
            remote(scales.at[c], scales.at[c], sc_sent, sc_came, sibling).start()
    lax.fori_loop(0, NZ, unpack_own, 0)
    arrived(scales.at[1 - c], sc_came)
    lax.fori_loop(0, NZ - 2, unpack_theirs, 0)
    arrived(sums.at[pl.ds(0, 7)], ey_recv)
    energy = functools.reduce(jnp.add, [sums[i] for i in range(12, 20)])
    mean = jnp.full((8, 128), jnp.sum(energy) / entries + 1e-06, f32)
    clip_out[...] = jnp.minimum(1.0, 1.0 / jnp.sqrt(mean))
    lax.fori_loop(NZ - 2, NZ, unpack_theirs, 0)

    sent(zb_send, az_sent)
    sent(zs_send, sz_sent)
    sent(blocks.at[0, pl.ds(0, 6)], ay_sent)
    sent(scales.at[0, pl.ds(0, 3)], sy_sent)
    sent(scales.at[0], sc_sent)
    sent(blocks.at[0], ac_sent)
    sent(sums.at[pl.ds(0, 3)], ex_send)
    sent(sums.at[pl.ds(0, 7)], ez_send)
    sent(sums.at[pl.ds(0, 7)], ey_send)


def reduced(acts, grad_out, projector, entries):
    sem = pltpu.SemaphoreType.DMA
    hbm = pl.BlockSpec(memory_space=pltpu.HBM)
    vmem = pl.BlockSpec(memory_space=pltpu.VMEM)
    return pl.pallas_call(
        functools.partial(reduce_kernel, entries),
        name="projected_gradient",
        out_shape=(jax.ShapeDtypeStruct((256, 2048), f32), jax.ShapeDtypeStruct((8, 128), f32)),
        in_specs=[hbm, hbm, hbm],
        out_specs=(vmem, vmem),
        scratch_shapes=[
            pltpu.VMEM((32, 256), bf16),
            pltpu.VMEM((1024, 2048), bf16),
            pltpu.VMEM((1024, 2048), bf16),
            pltpu.VMEM((2048, 128), bf16),
            pltpu.VMEM((128, 1024), f32),
            pltpu.VMEM((256, 1024), bf16),
            pltpu.VMEM((NZ, 128, 256), f32),
            pltpu.VMEM((NZ, NY - 1, 4, 16, 128), bf16),
            pltpu.VMEM((NZ, NY - 1, 4, 16, 128), bf16),
            pltpu.VMEM((NZ, NY - 1, 1, 128), f32),
            pltpu.VMEM((NZ, NY - 1, 1, 128), f32),
            pltpu.VMEM((NZ - 1, 4, 16, 128), bf16),
            pltpu.VMEM((NZ - 1, 4, 16, 128), bf16),
            pltpu.VMEM((NZ - 1, 1, 128), f32),
            pltpu.VMEM((NZ - 1, 1, 128), f32),
            pltpu.VMEM((2, NZ, NY, 4, 16, 128), bf16),
            pltpu.VMEM((2, NY, NZ, 1, 128), f32),
            pltpu.VMEM((20, 8, 128), f32),
            sem((3,)), sem((2,)), sem((2,)), sem, sem((NZ,)), sem, sem((NZ,)),
            sem, sem((NZ,)), sem, sem((NZ,)), sem, sem((NZ,)), sem, sem((NZ,)),
            sem, sem((NZ,)), sem, sem((NZ,)), sem, sem, sem, sem, sem, sem, sem, sem((NZ,)),
            sem, sem, sem, sem, sem, sem,
        ],
        compiler_params=pltpu.CompilerParams(
            collective_id=0, has_side_effects=True, vmem_limit_bytes=20 * 1024 * 1024
        ),
        cost_estimate=pl.CostEstimate(flops=1 << 31, bytes_accessed=6 << 20, transcendentals=1 << 20),
    )(acts, grad_out, projector)


def update_kernel(
    proj, clip, projector, first_old, second_old, update, first_new, second_new, u_out, f_out, s_out, sem
):
    scale = clip[:1, :]
    scale = jnp.concatenate([scale, scale], axis=1)
    rows = jnp.concatenate([projector[...], projector[...]], axis=1)
    copies = []

    def start(src, dst, i, j):
        cols = pl.ds(256 * i, 256)
        copies.append(pltpu.make_async_copy(src.at[:, cols], dst.at[:, cols], sem.at[i, j]))
        copies[-1].start()

    def project(i, high, low):
        moved = jnp.dot(rows, jnp.concatenate([high, low], axis=0), preferred_element_type=f32)
        u_out[:, pl.ds(256 * i, 256)] = galore_scale * moved

    waiting = None
    for i in range(8):
        cols = pl.ds(256 * i, 256)
        if i:
            project(i - 1, *waiting)
        clipped = scale * proj[:, cols]
        first = beta_one * first_old[:, cols] + (1.0 - beta_one) * clipped
        second = beta_two * second_old[:, cols] + (1.0 - beta_two) * clipped * clipped
        f_out[:, cols] = first
        s_out[:, cols] = second
        square = second * (1.0 / bias_two)
        direction = first * (1.0 / bias_one) / (square * lax.rsqrt(square) + 1e-08)
        high = direction.astype(bf16)
        waiting = (high, (direction - high.astype(f32)).astype(bf16))
        start(f_out, first_new, i, 0)
        start(s_out, second_new, i, 1)
        if i:
            start(u_out, update, i - 1, 2)
    project(7, *waiting)
    start(u_out, update, 7, 2)
    for copy in copies:
        copy.wait()


def updated(proj, clip, projector, moment_one, moment_two):
    hbm = pl.BlockSpec(memory_space=pltpu.HBM)
    vmem = pl.BlockSpec(memory_space=pltpu.VMEM)
    return pl.pallas_call(
        update_kernel,
        name="adam_update",
        out_shape=(
            jax.ShapeDtypeStruct((32, 2048), f32),
            jax.ShapeDtypeStruct((256, 2048), f32),
            jax.ShapeDtypeStruct((256, 2048), f32),
        ),
        in_specs=[vmem] * 5,
        out_specs=(hbm, hbm, hbm),
        scratch_shapes=[
            pltpu.VMEM((32, 2048), f32),
            pltpu.VMEM((256, 2048), f32),
            pltpu.VMEM((256, 2048), f32),
            pltpu.SemaphoreType.DMA((8, 3)),
        ],
        compiler_params=pltpu.CompilerParams(vmem_limit_bytes=16 * 1024 * 1024),
        cost_estimate=pl.CostEstimate(flops=1 << 26, bytes_accessed=10 << 20, transcendentals=1 << 20),
    )(proj, clip, projector, moment_one, moment_two)


def on_device(acts, grad_out, projector, moment_one, moment_two):
    entries = float(projector.shape[1] * grad_out.shape[1] * NX)
    acts, grad_out, rows = (pltpu.with_memory_space_constraint(a, pltpu.HBM) for a in (acts, grad_out, projector))
    proj, clip = reduced(acts, grad_out, rows, entries)
    return updated(proj, clip, projector, moment_one, moment_two)


def solution(mesh):
    placed = (P("dp", None), P("dp", "group"), P("dp", None), P(None, "group"), P(None, "group"))
    return jax.shard_map(
        on_device,
        mesh=mesh,
        in_specs=placed,
        out_specs=(P("dp", "group"), P(None, "group"), P(None, "group")),
        check_vma=False,
    )
```
